128 devices in a mesh: mp: 2 (over core), batch: 8 (over z, x_lo), vocab: 8 (over y, x_hi).
Axes of the slice: x: 4 (x_hi: 2, x_lo: 2; x = x_hi * 2 + x_lo), y: 4, z: 4, core: 2. Of those that a mesh axis runs over, the one named last changes fastest.
Arguments:
- hidden_teacher: bfloat16 [512, 4608], P(('batch', 'vocab'), 'mp'), may hold values from -6 to 6
- hidden_student: bfloat16 [512, 3584], P(('batch', 'vocab'), 'mp'), may hold values from -6 to 6
- teacher_weight: bfloat16 [4608, 131072], P('mp', ('batch', 'vocab')), may hold values from -0.4375 to 0.4375
- student_weight: bfloat16 [3584, 131072], P('mp', ('batch', 'vocab')), may hold values from -0.5 to 0.5
- token_weight: float32 [512], replicated, may hold values from 4 to 40
Outputs:
- divergence: float32 [512], replicated
- grad_hidden: bfloat16 [512, 3584], P(('batch', 'vocab'), 'mp')
- grad_weight: bfloat16 [3584, 131072], P('mp', ('batch', 'vocab'))
The draws below stay inside these ranges and needn't reach their ends.
All inputs are finite; a program needn't handle non-finite values.
Results may differ from the reference program's by a relative error of at most 0.005.
Values may be sent and summed in bfloat16 or wider, within the bound.
No kernel may reach another device: no remote copies, remote signals or barrier semaphores. Data moves between devices by JAX's collectives and lax.ppermute only.
A program may use at most 128 MiB of HBM per device.

```python
import math
import jax
import jax.numpy as jnp

DT = 4608
DS = 3584
TOKENS = 512
VOCAB = 131072


def shard_levels(key, shape, shards, least, top_value):
    def one(dim, shards_of):
        heights = jax.random.uniform(jax.random.fold_in(jax.random.fold_in(key, 6), dim), (shards_of,), jnp.float32, least / len(shards), top_value / len(shards))
        return jnp.repeat(jnp.exp(heights), shape[dim] // shards_of).reshape((-1,) + (1,) * (len(shape) - dim - 1))

    level = one(*shards[0])
    for cut in shards[1:]:
        level = level * one(*cut)
    return level


def normal_values(key, shape, spread, bound, shards=(), dtype=jnp.bfloat16):
    array = jax.random.normal(key, shape, jnp.float32) * spread
    if len(shards) > 0:
        array = shard_levels(key, shape, shards, -0.22, 0.18) * array
    return jnp.clip(array, min=-bound, max=bound).astype(dtype)


def setup_inputs(seed: int = 0) -> dict:
    streams_of = jax.random.split(jax.random.key(seed), 6)
    return {
        "hidden_teacher": normal_values(streams_of[0], (TOKENS, DT), 1.0, 6.0, ((0, 64), (1, 2))),
        "hidden_student": normal_values(streams_of[1], (TOKENS, DS), 1.0, 6.0, ((0, 64), (1, 2))),
        "teacher_weight": normal_values(streams_of[2], (DT, VOCAB), (DT // 25) ** -0.5, 0.4375, ((0, 2), (1, 64))),
        "student_weight": normal_values(streams_of[3], (DS, VOCAB), (DS // 25) ** -0.5, 0.5, ((0, 2), (1, 64))),
        "token_weight": jnp.clip(jnp.exp(jax.random.uniform(streams_of[4], (TOKENS,), jnp.float32, math.log(4.0), math.log(40.0))), 4.0, 40.0),
    }


softcap_limit = 30.0


def capped(values):
    return softcap_limit * jnp.tanh(values / softcap_limit)


def reference(hidden_teacher, hidden_student, teacher_weight, student_weight, token_weight):
    teacher_capped = capped(jnp.dot(hidden_teacher, teacher_weight, preferred_element_type=jnp.float32))
    student_capped = capped(jnp.dot(hidden_student, student_weight, preferred_element_type=jnp.float32))
    teacher_exp = jnp.exp(teacher_capped - softcap_limit)
    student_exp = jnp.exp(student_capped - softcap_limit)
    teacher_total = jnp.sum(teacher_exp, axis=1)
    student_total = jnp.sum(student_exp, axis=1)
    cross = jnp.sum(teacher_exp * (teacher_capped - student_capped), axis=1)
    divergence = cross / teacher_total - jnp.log(teacher_total) + jnp.log(student_total)
    slope = 1.0 - (student_capped / softcap_limit) ** 2
    probs_gap = student_exp / student_total[:, None] - teacher_exp / teacher_total[:, None]
    gap = (token_weight[:, None] * probs_gap * slope).astype(jnp.bfloat16)
    grad_hidden = jnp.dot(gap, student_weight.T, preferred_element_type=jnp.float32).astype(jnp.bfloat16)
    grad_weight = jnp.dot(hidden_student.T, gap, preferred_element_type=jnp.float32).astype(jnp.bfloat16)
    return divergence, grad_hidden, grad_weight
```

```python
import functools

import jax
import jax.numpy as jnp
import numpy as np
from jax import lax
from jax.experimental import pallas as pl
from jax.experimental.pallas import tpu as pltpu
from jax.sharding import PartitionSpec as P

softcap_limit = 30.0
tokens, teacher_width, student_width, vocab_local = 512, 2304, 1792, 2048
width = teacher_width + student_width
half = tokens // 2
everyone = ("mp", "batch", "vocab")
chips = ("batch", "vocab")
mega = 1024 * 1024

offsets = (0, 1, 3, 2)
stage_axes = (("y", "x"), ("x", "z"), ("z", "y"))


def place(index):
    core, z, x_lo, y, x_hi = np.unravel_index(index, (2, 4, 2, 4, 2))
    return {"core": int(core), "x": int(2 * x_hi + x_lo), "y": int(y), "z": int(z)}


def index_of(at):
    return int(
        np.ravel_multi_index(
            (at["core"], at["z"], at["x"] % 2, at["y"], at["x"] // 2), (2, 4, 2, 4, 2)
        )
    )


def moved(at, axis, by):
    return {**at, axis: (at[axis] + by) % 4}


def ring(axes, by):
    pairs = []
    for source in range(128):
        at = place(source)
        pairs.append((source, index_of(moved(at, axes[at["core"]], by))))
    return pairs


def send(block, axes, by):
    return lax.ppermute(block, everyone, ring(axes, by))


def swap(block):
    return lax.ppermute(block, "mp", [(0, 1), (1, 0)])


def row_table():
    table = np.zeros((128, 64), np.int32)
    for device in range(128):
        at = place(device)
        core = at["core"]
        for slot in range(64):
            owner = at
            for stage, digit in enumerate((slot % 4, slot // 4 % 4, slot // 16)):
                owner = moved(owner, stage_axes[stage][core], -offsets[digit])
            table[device, slot] = (index_of(owner) % 64 - 32 * core) % 64
    return table


def forward_first(order, x0, x1, x2, x3, teacher, student, rows, own, other):
    @pl.when(pl.program_id(0) == 0)
    def _():
        step = 512
        for at in range(0, width, step):
            cols = slice(at, at + step)
            block = jnp.concatenate([x[:, cols] for x in (x0, x1, x2, x3)], axis=0)
            rows[:, cols] = jnp.dot(
                order[...], block, preferred_element_type=jnp.float32
            ).astype(jnp.bfloat16)

    logits(rows, teacher, student, own, other)


def logits(rows, teacher, student, own, other):
    raw = jnp.dot(rows[:, :teacher_width], teacher[...], preferred_element_type=jnp.float32)
    own[0], other[0] = raw[:half], raw[half:]
    raw = jnp.dot(rows[:, teacher_width:], student[...], preferred_element_type=jnp.float32)
    own[1], other[1] = raw[:half], raw[half:]


def whole():
    return pl.BlockSpec(memory_space=pltpu.VMEM)


def forward(rows, teacher_weight, student_weight, chunk, n_chunks, tile=256):
    steps = vocab_local // n_chunks // tile
    at = lambda j: (0, chunk * steps + j)
    weights = [
        pl.BlockSpec((teacher_width, tile), at),
        pl.BlockSpec((student_width, tile), at),
    ]
    out = pl.BlockSpec((2, half, tile), lambda j: (0, 0, j))
    shape = jax.ShapeDtypeStruct((2, half, steps * tile), jnp.float32)
    params = pltpu.CompilerParams(vmem_limit_bytes=40 * mega)
    if chunk == 0:
        return pl.pallas_call(
            forward_first,
            grid=(steps,),
            in_specs=[whole()] * 5 + weights,
            out_specs=[whole(), out, out],
            out_shape=[jax.ShapeDtypeStruct((tokens, width), jnp.bfloat16), shape, shape],
            compiler_params=params,
        )(*rows, teacher_weight, student_weight)
    return pl.pallas_call(
        logits,
        grid=(steps,),
        in_specs=[whole()] + weights,
        out_specs=[out, out],
        out_shape=[shape, shape],
        compiler_params=params,
    )(rows, teacher_weight, student_weight)


def statistics_kernel(own, other, student_part, teacher_part, sums):
    @pl.when(pl.program_id(0) == 0)
    def _():
        sums[...] = jnp.zeros_like(sums)

    def lanes(values):
        total = values[:, :128]
        for at in range(128, values.shape[1], 128):
            total += values[:, at : at + 128]
        return total

    teacher_tanh = jnp.tanh((own[0] + other[0]) * (1.0 / softcap_limit))
    student_tanh = jnp.tanh((own[1] + other[1]) * (1.0 / softcap_limit))
    teacher_exp = jnp.exp(softcap_limit * teacher_tanh - softcap_limit)
    student_exp = jnp.exp(softcap_limit * student_tanh - softcap_limit)
    slope = 1.0 - student_tanh * student_tanh
    student_part[...] = student_exp * slope
    teacher_part[...] = teacher_exp * slope
    sums[0] += lanes(teacher_exp)
    sums[1] += lanes(student_exp)
    sums[2] += lanes(teacher_exp * (softcap_limit * (teacher_tanh - student_tanh)))


def statistics(own, other, tile=256):
    cols = own.shape[2]
    raw = pl.BlockSpec((2, half, tile), lambda j: (0, 0, j))
    part = pl.BlockSpec((half, tile), lambda j: (0, j))
    shape = jax.ShapeDtypeStruct((half, cols), jnp.float32)
    return pl.pallas_call(
        statistics_kernel,
        grid=(cols // tile,),
        in_specs=[raw, raw],
        out_specs=[part, part, whole()],
        out_shape=[shape, shape, jax.ShapeDtypeStruct((3, half, 128), jnp.float32)],
        compiler_params=pltpu.CompilerParams(vmem_limit_bytes=24 * mega),
    )(own, other)


def grad_hidden_kernel(order, own, other, weight, keep, send1, send2, send3, gap):
    @pl.when(pl.program_id(0) == 0)
    def _():
        step = 512
        for at in range(0, vocab_local, step):
            cols = slice(at, at + step)
            block = jnp.concatenate([own[:, cols], other[:, cols]], axis=0)
            gap[:, cols] = lax.dot_general(
                order[...], block, (((0,), (0,)), ((), ())), preferred_element_type=jnp.float32
            ).astype(jnp.bfloat16)

    term = lax.dot_general(
        gap[...], weight[...], (((1,), (1,)), ((), ())), preferred_element_type=jnp.float32
    )
    keep[...] = term[:128]
    send1[...] = term[128:256].astype(jnp.bfloat16)
    send2[...] = term[256:384].astype(jnp.bfloat16)
    send3[...] = term[384:].astype(jnp.bfloat16)


def grad_hidden_term(order, own, other, weight, tile=256):
    out = pl.BlockSpec((128, tile), lambda j: (0, j))
    return pl.pallas_call(
        grad_hidden_kernel,
        grid=(student_width // tile,),
        in_specs=[whole()] * 3 + [pl.BlockSpec((tile, vocab_local), lambda j: (j, 0))],
        out_specs=[out] * 4,
        out_shape=[jax.ShapeDtypeStruct((128, student_width), jnp.float32)]
        + [jax.ShapeDtypeStruct((128, student_width), jnp.bfloat16)] * 3,
        scratch_shapes=[pltpu.VMEM((tokens, vocab_local), jnp.bfloat16)],
        compiler_params=pltpu.CompilerParams(vmem_limit_bytes=24 * mega),
    )(order, own, other, weight)


def grad_weight_kernel(rows, own, other, out):
    over_rows = (((0,), (0,)), ((), ()))
    out[...] = (
        lax.dot_general(rows[:half], own[...], over_rows, preferred_element_type=jnp.float32)
        + lax.dot_general(rows[half:], other[...], over_rows, preferred_element_type=jnp.float32)
    ).astype(jnp.bfloat16)


def grad_weight_of(rows, own, other, tile=256):
    first = teacher_width // tile
    return pl.pallas_call(
        grad_weight_kernel,
        grid=(student_width // tile,),
        in_specs=[pl.BlockSpec((tokens, tile), lambda j: (0, first + j)), whole(), whole()],
        out_specs=pl.BlockSpec((tile, vocab_local), lambda j: (j, 0)),
        out_shape=jax.ShapeDtypeStruct((student_width, vocab_local), jnp.bfloat16),
        compiler_params=pltpu.CompilerParams(vmem_limit_bytes=24 * mega),
    )(rows, own, other)


def local(hidden_teacher, hidden_student, teacher_weight, student_weight, token_weight):
    core = lax.axis_index("mp")
    places = jnp.asarray(row_table())[lax.axis_index(everyone)]
    places = jnp.repeat(places * 8, 8) + jnp.tile(jnp.arange(8), 64)
    order = (jnp.arange(tokens)[:, None] == places[None, :]).astype(jnp.bfloat16)

    block = jnp.concatenate([hidden_teacher, hidden_student], axis=1)
    for axes in stage_axes[:2]:
        block = jnp.concatenate([block] + [send(block, axes, by) for by in offsets[1:]], axis=0)
    blocks = [block] + [send(block, stage_axes[2], by) for by in offsets[1:]]

    rows, own0, other0 = forward((order, *blocks), teacher_weight, student_weight, 0, 2)
    other0 = swap(other0)
    own1, other1 = forward(rows, teacher_weight, student_weight, 1, 2)
    other1 = swap(other1)
    student_part0, teacher_part0, sums0 = statistics(own0, other0)
    student_part1, teacher_part1, sums1 = statistics(own1, other1)
    sums = jnp.sum(sums0 + sums1, axis=2).reshape(6, 128)
    shared = lax.all_to_all(jnp.broadcast_to(sums[None], (64, 6, 128)), chips, 0, 0)
    teacher_total, student_total, cross = jnp.sum(shared, axis=0).reshape(3, half)

    weight_here = lax.dynamic_slice_in_dim(token_weight, core * half, half)
    student_scale = (weight_here / student_total)[:, None]
    teacher_scale = (weight_here / teacher_total)[:, None]
    gap = jnp.concatenate(
        [
            (student_part0 * student_scale - teacher_part0 * teacher_scale).astype(jnp.bfloat16),
            (student_part1 * student_scale - teacher_part1 * teacher_scale).astype(jnp.bfloat16),
        ],
        axis=1,
    )
    gap_other = swap(gap)

    keep, *sends = grad_hidden_term(order, gap, gap_other, student_weight)
    received = [send(b, stage_axes[2], -by) for b, by in zip(sends, offsets[1:])]
    grad_weight = grad_weight_of(rows, gap, gap_other)
    total = keep + sum(r.astype(jnp.float32) for r in received)
    for axes in stage_axes[1::-1]:
        size = total.shape[0] // 4
        parts = [total[i * size : (i + 1) * size] for i in range(4)]
        received = [send(p, axes, -by) for p, by in zip(parts[1:], offsets[1:])]
        total = parts[0] + sum(received)
    grad_hidden = total.astype(jnp.bfloat16)

    divergence = cross / teacher_total - jnp.log(teacher_total) + jnp.log(student_total)
    divergence_other = swap(divergence)
    divergence = jnp.where(
        core == 0,
        jnp.concatenate([divergence, divergence_other]),
        jnp.concatenate([divergence_other, divergence]),
    )
    return (divergence, grad_hidden, grad_weight)


def solution(mesh):
    placed = (
        P(("batch", "vocab"), "mp"),
        P(("batch", "vocab"), "mp"),
        P("mp", ("batch", "vocab")),
        P("mp", ("batch", "vocab")),
        P(),
    )
    return jax.shard_map(
        local,
        mesh=mesh,
        in_specs=placed,
        out_specs=(P(), P(("batch", "vocab"), "mp"), P("mp", ("batch", "vocab"))),
        check_vma=False,
    )
```

```python
import functools

import jax
import jax.numpy as jnp
import numpy as np
from jax import lax
from jax.experimental import pallas as pl
from jax.experimental.pallas import tpu as pltpu
from jax.sharding import PartitionSpec as P

softcap_limit = 30.0
tokens, teacher_width, student_width, vocab_local = 512, 2304, 1792, 2048
width = teacher_width + student_width
half = tokens // 2
everyone = ("mp", "batch", "vocab")
mega = 1024 * 1024

offsets = (0, 1, 3, 2)
teacher_axes = (("y", "z"), ("x", "x"), ("z", "y"))
student_axes = (("y", "z"), ("z", "y"), ("x", "x"))
reduce_axes = (("z", "y"), ("x", "z"), ("y", "x"))


def place(index):
    core, z, x_lo, y, x_hi = np.unravel_index(index, (2, 4, 2, 4, 2))
    return {"core": int(core), "x": int(2 * x_hi + x_lo), "y": int(y), "z": int(z)}


def index_of(at):
    return int(
        np.ravel_multi_index(
            (at["core"], at["z"], at["x"] % 2, at["y"], at["x"] // 2), (2, 4, 2, 4, 2)
        )
    )


def moved(at, axis, by):
    return {**at, axis: (at[axis] + by) % 4}


def ring(axes, by):
    pairs = []
    for source in range(128):
        at = place(source)
        pairs.append((source, index_of(moved(at, axes[at["core"]], by))))
    return pairs


def send(block, axes, by):
    return lax.ppermute(block, everyone, ring(axes, by))


def swap(block):
    return lax.ppermute(block, "mp", [(0, 1), (1, 0)])


def row_table(axes_of):
    table = np.zeros((128, 64), np.int32)
    for device in range(128):
        at = place(device)
        core = at["core"]
        for slot in range(64):
            owner = at
            for stage, digit in enumerate((slot % 4, slot // 4 % 4, slot // 16)):
                owner = moved(owner, axes_of[stage][core], -offsets[digit])
            table[device, slot] = (index_of(owner) % 64 - 32 * core) % 64
    return table


def gathered(order, blocks, rows):
    step = 256
    for at in range(0, rows.shape[1], step):
        cols = slice(at, at + step)
        block = jnp.concatenate([x[:, cols] for x in blocks], axis=0)
        rows[:, cols] = jnp.dot(
            order[...], block, preferred_element_type=jnp.float32
        ).astype(jnp.bfloat16)


def first_kernel(order, x0, x1, x2, x3, weight, own, other, rows):
    @pl.when(pl.program_id(0) == 0)
    def _():
        gathered(order, (x0, x1, x2, x3), rows)

    next_kernel(rows, weight, own, other)


def next_kernel(rows, weight, own, other):
    raw = jnp.dot(rows[...], weight[...], preferred_element_type=jnp.float32)
    own[...], other[...] = raw[:half], raw[half:]


def setup_kernel(tables, token_weight, teacher_order, student_order, reduce_order, weight_here, first_core):
    me = lax.axis_index(everyone)
    core = lax.axis_index("mp")
    for i, order in enumerate((teacher_order, student_order, reduce_order)):
        places = tables[i, pl.ds(me, 1), :]
        rows = lax.broadcasted_iota(jnp.int32, (tokens, tokens), 0)
        order[...] = jnp.where(rows == places, 1.0, 0.0).astype(jnp.bfloat16)
    weight_here[...] = token_weight[pl.ds(core * 2, 2), :]
    first_core[...] = jnp.full(first_core.shape, 1.0, jnp.float32) * (core == 0).astype(jnp.float32)


def setup(token_weight):
    tables = np.stack([row_table(a) for a in (teacher_axes, student_axes, reduce_axes[::-1])])
    tables = np.repeat(tables * 8, 8, axis=2) + np.tile(np.arange(8, dtype=np.int32), 64)
    order = jax.ShapeDtypeStruct((tokens, tokens), jnp.bfloat16)
    small = jax.ShapeDtypeStruct((2, 128), jnp.float32)
    return pl.pallas_call(
        setup_kernel,
        in_specs=[whole()] * 2,
        out_specs=[whole()] * 5,
        out_shape=[order] * 3 + [small] * 2,
        compiler_params=pltpu.CompilerParams(vmem_limit_bytes=4 * mega),
        cost_estimate=cost(0, 24 * mega),
    )(jnp.asarray(tables.astype(np.int32)), token_weight.reshape(4, 128))


def cost(macs, moved, transcendentals=0):
    return pl.CostEstimate(flops=2 * macs, bytes_accessed=moved, transcendentals=transcendentals)


def whole():
    return pl.BlockSpec(memory_space=pltpu.VMEM)


def forward(rows, weight, chunk, n_chunks, keep_rows=False, tile=256, limit=8):
    steps = vocab_local // n_chunks // tile
    depth = weight.shape[0]
    weight_spec = pl.BlockSpec((depth, tile), lambda j: (0, chunk * steps + j))
    out = pl.BlockSpec((half, tile), lambda j: (0, j))
    shape = jax.ShapeDtypeStruct((half, steps * tile), jnp.float32)
    held = jax.ShapeDtypeStruct((tokens, depth), jnp.bfloat16)
    params = pltpu.CompilerParams(vmem_limit_bytes=limit * mega)
    work = cost(tokens * depth * steps * tile, (2 * depth + 4 * tokens) * steps * tile)
    if chunk == 0:
        return pl.pallas_call(
            first_kernel,
            grid=(steps,),
            in_specs=[whole()] * 5 + [weight_spec],
            out_specs=[out, out] + [whole()] * keep_rows,
            out_shape=[shape, shape] + [held] * keep_rows,
            scratch_shapes=[] if keep_rows else [pltpu.VMEM(held.shape, held.dtype)],
            compiler_params=params,
            cost_estimate=work,
        )(*rows, weight)
    return pl.pallas_call(
        next_kernel,
        grid=(steps,),
        in_specs=[whole(), weight_spec],
        out_specs=[out, out],
        out_shape=[shape, shape],
        compiler_params=params,
        cost_estimate=work,
    )(rows, weight)


def lanes(values):
    total = values[:, :128]
    for at in range(128, values.shape[1], 128):
        total += values[:, at : at + 128]
    return total


def statistics_kernel(last, before, t_own, t_other, s_own, s_other, student_part, teacher_part, out, sums):
    @pl.when(pl.program_id(0) == 0)
    def _():
        sums[...] = before[...] if last else jnp.zeros_like(sums)

    teacher_tanh = jnp.tanh((t_own[...] + t_other[...]) * (1.0 / softcap_limit))
    student_tanh = jnp.tanh((s_own[...] + s_other[...]) * (1.0 / softcap_limit))
    teacher_exp = jnp.exp(softcap_limit * teacher_tanh - softcap_limit)
    student_exp = jnp.exp(softcap_limit * student_tanh - softcap_limit)
    slope = 1.0 - student_tanh * student_tanh
    student_part[...] = student_exp * slope
    teacher_part[...] = teacher_exp * slope
    sums[0] += lanes(teacher_exp)
    sums[1] += lanes(student_exp)
    sums[2] += lanes(teacher_exp * (softcap_limit * (teacher_tanh - student_tanh)))

    @pl.when(pl.program_id(0) == pl.num_programs(0) - 1)
    def _():
        if last:
            rows = [
                jnp.sum(sums[i, at : at + 128].T, axis=0, keepdims=True)
                for i in range(3)
                for at in (0, 128)
            ]
            out[...] = jnp.concatenate(rows + [jnp.zeros((2, 128), jnp.float32)], axis=0)
        else:
            out[...] = sums[...]


def statistics(teacher, student, chunk, before=None, tile=256):
    cols = student[0].shape[1]
    steps = cols // tile
    last = before is not None
    from_teacher = pl.BlockSpec((half, tile), lambda j: (0, chunk * steps + j))
    part = pl.BlockSpec((half, tile), lambda j: (0, j))
    shape = jax.ShapeDtypeStruct((half, cols), jnp.float32)
    sums = (3, half, 128)
    kernel = functools.partial(statistics_kernel, last)
    if not last:
        kernel = functools.partial(statistics_kernel, last, None)
    return pl.pallas_call(
        kernel,
        grid=(steps,),
        in_specs=[whole()] * last + [from_teacher] * 2 + [part] * 2,
        out_specs=[part, part, whole()],
        out_shape=[
            shape,
            shape,
            jax.ShapeDtypeStruct((8, 128) if last else sums, jnp.float32),
        ],
        scratch_shapes=[pltpu.VMEM(sums, jnp.float32)],
        compiler_params=pltpu.CompilerParams(vmem_limit_bytes=7 * mega),
        cost_estimate=cost(10 * half * cols, 24 * half * cols, 4 * half * cols),
    )(*([before] if last else []), *teacher, *student)


def gap_kernel(total, token_weight, student0, teacher0, student1, teacher1, gap, divergence):
    teacher_total, student_total, cross = total[0:2], total[2:4], total[4:6]
    divergence[...] = cross / teacher_total - jnp.log(teacher_total) + jnp.log(student_total)
    rows = [token_weight[...] / student_total, token_weight[...] / teacher_total, total[0:4]]
    scales = jnp.concatenate(rows, axis=0).T
    cols = student0.shape[1]
    for i in range(2):
        at = slice(128 * i, 128 * (i + 1))
        student_scale, teacher_scale = scales[:, i : i + 1], scales[:, 2 + i : 3 + i]
        for first, student, teacher in ((0, student0, teacher0), (cols, student1, teacher1)):
            gap[at, first : first + cols] = (
                student[at] * student_scale - teacher[at] * teacher_scale
            ).astype(jnp.bfloat16)


def gap_of(total, token_weight, parts):
    return pl.pallas_call(
        gap_kernel,
        in_specs=[whole()] * 6,
        out_specs=[whole(), whole()],
        out_shape=[
            jax.ShapeDtypeStruct((half, vocab_local), jnp.bfloat16),
            jax.ShapeDtypeStruct((2, 128), jnp.float32),
        ],
        compiler_params=pltpu.CompilerParams(vmem_limit_bytes=4 * mega),
        cost_estimate=cost(2 * half * vocab_local, 10 * half * vocab_local),
    )(total, token_weight, *parts)


def grad_hidden_kernel(order, own, other, weight, keep, send1, send2, send3, gap):
    @pl.when(pl.program_id(0) == 0)
    def _():
        step = 512
        for at in range(0, vocab_local, step):
            cols = slice(at, at + step)
            block = jnp.concatenate([own[:, cols], other[:, cols]], axis=0)
            gap[:, cols] = lax.dot_general(
                order[...], block, (((0,), (0,)), ((), ())), preferred_element_type=jnp.float32
            ).astype(jnp.bfloat16)

    term = lax.dot_general(
        gap[...], weight[...], (((1,), (1,)), ((), ())), preferred_element_type=jnp.float32
    )
    keep[...] = term[:128]
    send1[...] = term[128:256].astype(jnp.bfloat16)
    send2[...] = term[256:384].astype(jnp.bfloat16)
    send3[...] = term[384:].astype(jnp.bfloat16)


def grad_hidden_term(order, own, other, weight, tile=256):
    out = pl.BlockSpec((128, tile), lambda j: (0, j))
    return pl.pallas_call(
        grad_hidden_kernel,
        grid=(student_width // tile,),
        in_specs=[whole()] * 3 + [pl.BlockSpec((tile, vocab_local), lambda j: (j, 0))],
        out_specs=[out] * 4,
        out_shape=[jax.ShapeDtypeStruct((128, student_width), jnp.float32)]
        + [jax.ShapeDtypeStruct((128, student_width), jnp.bfloat16)] * 3,
        scratch_shapes=[pltpu.VMEM((tokens, vocab_local), jnp.bfloat16)],
        compiler_params=pltpu.CompilerParams(vmem_limit_bytes=8 * mega),
        cost_estimate=cost(tokens * student_width * vocab_local, 2 * student_width * vocab_local),
    )(order, own, other, weight)


def grad_weight_kernel(rows, own, other, out):
    over_rows = (((0,), (0,)), ((), ()))
    out[...] = (
        lax.dot_general(rows[:half], own[...], over_rows, preferred_element_type=jnp.float32)
        + lax.dot_general(rows[half:], other[...], over_rows, preferred_element_type=jnp.float32)
    ).astype(jnp.bfloat16)


def grad_weight_of(rows, own, other, tile=256):
    return pl.pallas_call(
        grad_weight_kernel,
        grid=(student_width // tile,),
        in_specs=[pl.BlockSpec((tokens, tile), lambda j: (0, j)), whole(), whole()],
        out_specs=pl.BlockSpec((tile, vocab_local), lambda j: (j, 0)),
        out_shape=jax.ShapeDtypeStruct((student_width, vocab_local), jnp.bfloat16),
        compiler_params=pltpu.CompilerParams(vmem_limit_bytes=8 * mega),
        cost_estimate=cost(tokens * student_width * vocab_local, 2 * student_width * vocab_local),
    )(rows, own, other)


def local(hidden_teacher, hidden_student, teacher_weight, student_weight, token_weight):
    teacher_order, student_order, reduce_order, weight_here, first_core = setup(token_weight)

    def shared_along(block, axes):
        return [block] + [send(block, axes, by) for by in offsets[1:]]

    def joined(blocks):
        return jnp.concatenate(blocks, axis=0)

    block = joined(
        shared_along(jnp.concatenate([hidden_teacher, hidden_student], axis=1), teacher_axes[0])
    )
    teacher, student = block[:, :teacher_width], block[:, teacher_width:]
    student = joined(shared_along(student, student_axes[1]))
    teacher = joined(shared_along(teacher, teacher_axes[1]))
    teacher, student = lax.optimization_barrier((teacher, student))
    teacher = shared_along(teacher, teacher_axes[2])
    student = shared_along(student, student_axes[2])

    teacher_own, teacher_other = forward((teacher_order, *teacher), teacher_weight, 0, 1)
    teacher_other, student[1], student[2], student[3] = lax.optimization_barrier(
        (teacher_other, student[1], student[2], student[3])
    )
    teacher_raw = (teacher_own, swap(teacher_other))
    own, other, rows = forward((student_order, *student), student_weight, 0, 2, keep_rows=True)
    student_raw0 = (own, swap(other))
    own, other = forward(rows, student_weight, 1, 2)
    student_raw1 = (own, swap(other))
    student_part0, teacher_part0, sums = statistics(teacher_raw, student_raw0, 0)
    student_part1, teacher_part1, sums = statistics(teacher_raw, student_raw1, 1, sums)
    for axes in reduce_axes:
        sums = sum(shared_along(sums, axes))
    gap, divergence = gap_of(
        sums, weight_here, (student_part0, teacher_part0, student_part1, teacher_part1)
    )
    gap_other = swap(gap)

    keep, *sends = grad_hidden_term(reduce_order, gap, gap_other, student_weight)
    received = [send(b, reduce_axes[0], -by) for b, by in zip(sends, offsets[1:])]
    divergence_other = swap(divergence)
    grad_weight = grad_weight_of(rows, gap, gap_other)
    keep, grad_weight, divergence_other = lax.optimization_barrier(
        (keep, grad_weight, divergence_other)
    )
    total = keep + sum(r.astype(jnp.float32) for r in received)
    for axes, kind in zip(reduce_axes[1:], (jnp.bfloat16, jnp.float32)):
        size = total.shape[0] // 4
        parts = [total[i * size : (i + 1) * size] for i in range(4)]
        received = [send(p.astype(kind), axes, -by) for p, by in zip(parts[1:], offsets[1:])]
        total = parts[0] + sum(r.astype(jnp.float32) for r in received)
    grad_hidden = total.astype(jnp.bfloat16)

    first_core = first_core > 0.5
    divergence = jnp.concatenate(
        [
            jnp.where(first_core, divergence, divergence_other),
            jnp.where(first_core, divergence_other, divergence),
        ]
    ).reshape(tokens)
    return (divergence, grad_hidden, grad_weight)


def solution(mesh):
    placed = (
        P(("batch", "vocab"), "mp"),
        P(("batch", "vocab"), "mp"),
        P("mp", ("batch", "vocab")),
        P("mp", ("batch", "vocab")),
        P(),
    )
    return jax.shard_map(
        local,
        mesh=mesh,
        in_specs=placed,
        out_specs=(P(), P(("batch", "vocab"), "mp"), P("mp", ("batch", "vocab"))),
        check_vma=False,
    )
```

```python
import functools

import jax
import jax.numpy as jnp
import numpy as np
from jax import lax
from jax.experimental import pallas as pl
from jax.experimental.pallas import tpu as pltpu
from jax.sharding import PartitionSpec as P

softcap_limit = 30.0
tokens, teacher_width, student_width, vocab_local = 512, 2304, 1792, 2048
width = teacher_width + student_width
half = tokens // 2
apart = 1536
everyone = ("mp", "batch", "vocab")
mega = 1024 * 1024

offsets = (0, 1, 3, 2)
main_axes = (("y", "z"), ("x", "x"), ("z", "y"))
apart_axes = (("y", "z"), ("z", "y"), ("x", "x"))
reduce_axes = (("z", "y"), ("x", "z"), ("y", "x"))


def place(index):
    core, z, x_lo, y, x_hi = np.unravel_index(index, (2, 4, 2, 4, 2))
    return {"core": int(core), "x": int(2 * x_hi + x_lo), "y": int(y), "z": int(z)}


def index_of(at):
    return int(
        np.ravel_multi_index(
            (at["core"], at["z"], at["x"] % 2, at["y"], at["x"] // 2), (2, 4, 2, 4, 2)
        )
    )


def moved(at, axis, by):
    return {**at, axis: (at[axis] + by) % 4}


def ring(axes, by):
    pairs = []
    for source in range(128):
        at = place(source)
        pairs.append((source, index_of(moved(at, axes[at["core"]], by))))
    return pairs


def send(block, axes, by):
    return lax.ppermute(block, everyone, ring(axes, by))


def swap(block):
    return lax.ppermute(block, "mp", [(0, 1), (1, 0)])


def side_by_side_kernel(teacher, student, out, held_teacher, held_student, arrived):
    copies = [
        pltpu.make_async_copy(teacher, held_teacher, arrived.at[0]),
        pltpu.make_async_copy(student, held_student, arrived.at[1]),
    ]
    for copy in copies:
        copy.start()
    for copy in copies:
        copy.wait()
    out[:, :apart] = held_student[:, :apart]
    out[:, apart : apart + teacher_width] = held_teacher[...]
    out[:, apart + teacher_width :] = held_student[:, apart:]


def side_by_side(teacher, student):
    return pl.pallas_call(
        side_by_side_kernel,
        in_specs=[pl.BlockSpec(memory_space=pl.ANY)] * 2,
        out_specs=whole(),
        out_shape=jax.ShapeDtypeStruct((teacher.shape[0], width), teacher.dtype),
        scratch_shapes=[
            pltpu.VMEM(teacher.shape, teacher.dtype),
            pltpu.VMEM(student.shape, student.dtype),
            pltpu.SemaphoreType.DMA((2,)),
        ],
        compiler_params=pltpu.CompilerParams(vmem_limit_bytes=mega),
        cost_estimate=cost(0, 4 * teacher.shape[0] * width),
    )(teacher, student)


def gathered(order, blocks, first, rows):
    step = 256
    for at in range(0, rows.shape[1], step):
        cols = slice(first + at, first + at + step)
        block = jnp.concatenate([x[:, cols] for x in blocks], axis=0)
        rows[:, at : at + step] = jnp.dot(
            order[...], block, preferred_element_type=jnp.float32
        ).astype(jnp.bfloat16)


def logits(rows, weight, first, own, other):
    step = 512
    for at in range(0, own.shape[1], step):
        raw = jnp.dot(
            rows[...], weight[:, first + at : first + at + step], preferred_element_type=jnp.float32
        )
        own[:, at : at + step], other[:, at : at + step] = raw[:half], raw[half:]


def teacher_kernel(order, x0, x1, x2, x3, weight, own, other, rows):
    gathered(order, (x0, x1, x2, x3), 0, rows)
    logits(rows, weight, 0, own, other)


def student_kernel(main_order, apart_order, *refs):
    main, separate, (weight, own, other, rows) = refs[:4], refs[4:8], refs[8:]
    gathered(apart_order, separate, 0, rows.at[:, :apart])
    gathered(main_order, main, teacher_width, rows.at[:, apart:])
    logits(rows, weight, 0, own, other)


def student_rest_kernel(rows, weight, own, other):
    logits(rows, weight, vocab_local - own.shape[1], own, other)


def own_place(token, at, axes_of, core):
    block, row = token // 8, token % 8
    for stage, axes in enumerate(axes_of):
        digit = (block >> (2 * stage)) & 3
        offset = digit ^ (digit >> 1)
        for axis in at:
            taken = (axes[0] == axis) * (1 - core) + (axes[1] == axis) * core
            at[axis] = at[axis] - taken * offset
    x, y, z = (at[axis] & 3 for axis in "xyz")
    owner = z * 16 + (x & 1) * 8 + y * 2 + (x >> 1)
    return ((owner - 32 * core) & 63) * 8 + row


def setup_kernel(token_weight, _, main_order, apart_order, reduce_order, weight_here, first_core):
    core = lax.axis_index("mp")
    batch, vocab = lax.axis_index("batch"), lax.axis_index("vocab")
    at = {"x": (vocab % 2) * 2 + batch % 2, "y": vocab // 2, "z": batch // 2}
    token = lax.broadcasted_iota(jnp.int32, (1, tokens), 1)
    rows = lax.broadcasted_iota(jnp.int32, (tokens, tokens), 0)
    for order, axes_of in (
        (main_order, main_axes),
        (apart_order, apart_axes),
        (reduce_order, reduce_axes[::-1]),
    ):
        places = own_place(token, dict(at), axes_of, core)
        order[...] = jnp.where(rows == places, 1.0, 0.0).astype(jnp.bfloat16)
    weight_here[...] = token_weight[pl.ds(core * 2, 2), :]
    first_core[...] = jnp.full(first_core.shape, 1.0, jnp.float32) * (core == 0).astype(jnp.float32)


def setup(token_weight, weight):
    order = jax.ShapeDtypeStruct((tokens, tokens), jnp.bfloat16)
    small = jax.ShapeDtypeStruct((2, 128), jnp.float32)
    return pl.pallas_call(
        setup_kernel,
        in_specs=[whole(), pl.BlockSpec(memory_space=pl.ANY)],
        out_specs=[whole()] * 5,
        out_shape=[order] * 3 + [small] * 2,
        compiler_params=pltpu.CompilerParams(vmem_limit_bytes=4 * mega),
        cost_estimate=cost(0, 2 * mega),
    )(token_weight.reshape(4, 128), weight)


def cost(macs, moved, transcendentals=0):
    return pl.CostEstimate(flops=2 * macs, bytes_accessed=moved, transcendentals=transcendentals)


def whole():
    return pl.BlockSpec(memory_space=pltpu.VMEM)


def raw_shapes(cols):
    return [jax.ShapeDtypeStruct((half, cols), jnp.float32)] * 2


def teacher_logits(order, blocks, weight):
    return pl.pallas_call(
        teacher_kernel,
        in_specs=[whole()] * 6,
        out_specs=[whole()] * 2,
        out_shape=raw_shapes(vocab_local),
        scratch_shapes=[pltpu.VMEM((tokens, teacher_width), jnp.bfloat16)],
        compiler_params=pltpu.CompilerParams(vmem_limit_bytes=24 * mega),
        cost_estimate=cost(tokens * weight.size, 2 * weight.size),
    )(order, *blocks, weight)


def student_logits(main_order, apart_order, main, separate, weight, cols):
    return pl.pallas_call(
        student_kernel,
        in_specs=[whole()] * 11,
        out_specs=[whole()] * 3,
        out_shape=raw_shapes(cols) + [jax.ShapeDtypeStruct((tokens, student_width), jnp.bfloat16)],
        compiler_params=pltpu.CompilerParams(vmem_limit_bytes=20 * mega),
        cost_estimate=cost(tokens * student_width * cols, 2 * weight.size),
    )(main_order, apart_order, *main, *separate, weight)


def student_rest(rows, weight, cols):
    return pl.pallas_call(
        student_rest_kernel,
        in_specs=[whole()] * 2,
        out_specs=[whole()] * 2,
        out_shape=raw_shapes(cols),
        compiler_params=pltpu.CompilerParams(vmem_limit_bytes=16 * mega),
        cost_estimate=cost(tokens * student_width * cols, 2 * weight.size),
    )(rows, weight)


def lanes(values):
    total = values[:, :128]
    for at in range(128, values.shape[1], 128):
        total += values[:, at : at + 128]
    return total


def statistics_kernel(last, before, t_own, t_other, s_own, s_other, student_part, teacher_part, out, sums):
    @pl.when(pl.program_id(0) == 0)
    def _():
        sums[...] = before[...] if last else jnp.zeros_like(sums)

    teacher_tanh = jnp.tanh((t_own[...] + t_other[...]) * (1.0 / softcap_limit))
    student_tanh = jnp.tanh((s_own[...] + s_other[...]) * (1.0 / softcap_limit))
    teacher_exp = jnp.exp(softcap_limit * teacher_tanh - softcap_limit)
    student_exp = jnp.exp(softcap_limit * student_tanh - softcap_limit)
    slope = 1.0 - student_tanh * student_tanh
    student_part[...] = student_exp * slope
    teacher_part[...] = teacher_exp * slope
    sums[0] += lanes(teacher_exp)
    sums[1] += lanes(student_exp)
    sums[2] += lanes(teacher_exp * (softcap_limit * (teacher_tanh - student_tanh)))

    @pl.when(pl.program_id(0) == pl.num_programs(0) - 1)
    def _():
        if last:
            rows = [
                jnp.sum(sums[i, at : at + 128].T, axis=0, keepdims=True)
                for i in range(3)
                for at in (0, 128)
            ]
            out[...] = jnp.concatenate(rows + [jnp.zeros((2, 128), jnp.float32)], axis=0)
        else:
            out[...] = sums[...]


def statistics(teacher, student, chunk, before=None, tile=256):
    cols = student[0].shape[1]
    steps = cols // tile
    last = before is not None
    from_teacher = pl.BlockSpec((half, tile), lambda j: (0, chunk * steps + j))
    part = pl.BlockSpec((half, tile), lambda j: (0, j))
    shape = jax.ShapeDtypeStruct((half, cols), jnp.float32)
    sums = (3, half, 128)
    kernel = functools.partial(statistics_kernel, last)
    if not last:
        kernel = functools.partial(statistics_kernel, last, None)
    return pl.pallas_call(
        kernel,
        grid=(steps,),
        in_specs=[whole()] * last + [from_teacher] * 2 + [part] * 2,
        out_specs=[part, part, whole()],
        out_shape=[
            shape,
            shape,
            jax.ShapeDtypeStruct((8, 128) if last else sums, jnp.float32),
        ],
        scratch_shapes=[pltpu.VMEM(sums, jnp.float32)],
        compiler_params=pltpu.CompilerParams(vmem_limit_bytes=7 * mega),
        cost_estimate=cost(10 * half * cols, 24 * half * cols, 4 * half * cols),
    )(*([before] if last else []), *teacher, *student)


def gap_kernel(total, token_weight, student0, teacher0, student1, teacher1, gap, divergence):
    teacher_total, student_total, cross = total[0:2], total[2:4], total[4:6]
    divergence[...] = cross / teacher_total - jnp.log(teacher_total) + jnp.log(student_total)
    rows = [token_weight[...] / student_total, token_weight[...] / teacher_total, total[0:4]]
    scales = jnp.concatenate(rows, axis=0).T
    cols = student0.shape[1]
    for i in range(2):
        at = slice(128 * i, 128 * (i + 1))
        student_scale, teacher_scale = scales[:, i : i + 1], scales[:, 2 + i : 3 + i]
        for first, student, teacher in ((0, student0, teacher0), (cols, student1, teacher1)):
            gap[at, first : first + cols] = (
                student[at] * student_scale - teacher[at] * teacher_scale
            ).astype(jnp.bfloat16)


def gap_of(total, token_weight, parts):
    return pl.pallas_call(
        gap_kernel,
        in_specs=[whole()] * 6,
        out_specs=[whole(), whole()],
        out_shape=[
            jax.ShapeDtypeStruct((half, vocab_local), jnp.bfloat16),
            jax.ShapeDtypeStruct((2, 128), jnp.float32),
        ],
        compiler_params=pltpu.CompilerParams(vmem_limit_bytes=4 * mega),
        cost_estimate=cost(2 * half * vocab_local, 10 * half * vocab_local),
    )(total, token_weight, *parts)


part = student_width // 2


def hidden_term(gap, weight, keep, sends):
    term = lax.dot_general(gap, weight, (((1,), (1,)), ((), ())), preferred_element_type=jnp.float32)
    keep[...] = term[:128]
    for i, send in enumerate(sends):
        send[...] = term[128 * (i + 1) : 128 * (i + 2)].astype(jnp.bfloat16)


def hidden_first_kernel(order, own, other, weight, gap, keep, *sends):
    step = 512
    for at in range(0, vocab_local, step):
        cols = slice(at, at + step)
        block = jnp.concatenate([own[:, cols], other[:, cols]], axis=0)
        gap[:, cols] = lax.dot_general(
            order[...], block, (((0,), (0,)), ((), ())), preferred_element_type=jnp.float32
        ).astype(jnp.bfloat16)
    hidden_term(gap[...], weight[:part], keep, sends)


def hidden_second_kernel(gap, weight, keep, *sends):
    hidden_term(gap[...], weight[part:], keep, sends)


def hidden_shapes():
    return [jax.ShapeDtypeStruct((128, part), jnp.float32)] + [
        jax.ShapeDtypeStruct((128, part), jnp.bfloat16)
    ] * 3


def hidden_first(order, own, other, weight):
    return pl.pallas_call(
        hidden_first_kernel,
        in_specs=[whole()] * 4,
        out_specs=[whole()] * 5,
        out_shape=[jax.ShapeDtypeStruct((tokens, vocab_local), jnp.bfloat16)] + hidden_shapes(),
        compiler_params=pltpu.CompilerParams(vmem_limit_bytes=20 * mega),
        cost_estimate=cost(tokens * weight.size // 2, weight.size),
    )(order, own, other, weight)


def hidden_second(gap, weight):
    return pl.pallas_call(
        hidden_second_kernel,
        in_specs=[whole()] * 2,
        out_specs=[whole()] * 4,
        out_shape=hidden_shapes(),
        compiler_params=pltpu.CompilerParams(vmem_limit_bytes=18 * mega),
        cost_estimate=cost(tokens * weight.size // 2, weight.size),
    )(gap, weight)


def total_of(keep, received, at, size):
    rows = pl.ds(at, size)
    return keep[rows] + sum(r[rows].astype(jnp.float32) for r in received)


def first_sum_kernel(*refs):
    halves, (keep, *sends) = (refs[:4], refs[4:8]), refs[8:]
    for i, (mine, *received) in enumerate(halves):
        cols = slice(i * part, (i + 1) * part)
        keep[:, cols] = total_of(mine, received, 0, 32)
        for j, send in enumerate(sends):
            send[:, cols] = total_of(mine, received, 32 * (j + 1), 32).astype(send.dtype)


def first_sum(halves):
    shape = (32, student_width)
    return pl.pallas_call(
        first_sum_kernel,
        in_specs=[whole()] * 8,
        out_specs=[whole()] * 4,
        out_shape=[jax.ShapeDtypeStruct(shape, jnp.float32)]
        + [jax.ShapeDtypeStruct(shape, jnp.bfloat16)] * 3,
        compiler_params=pltpu.CompilerParams(vmem_limit_bytes=6 * mega),
        cost_estimate=cost(128 * student_width * 4, 2 * mega),
    )(*halves[0], *halves[1])


def second_sum_kernel(mine, *refs):
    received, (keep, *sends) = refs[:3], refs[3:]
    total = mine[...] + sum(r[...].astype(jnp.float32) for r in received)
    keep[...] = total[:8]
    for j, send in enumerate(sends):
        send[...] = total[8 * (j + 1) : 8 * (j + 2)]


def second_sum(mine, received):
    return pl.pallas_call(
        second_sum_kernel,
        in_specs=[whole()] * 4,
        out_specs=[whole()] * 4,
        out_shape=[jax.ShapeDtypeStruct((8, student_width), jnp.float32)] * 4,
        compiler_params=pltpu.CompilerParams(vmem_limit_bytes=3 * mega),
        cost_estimate=cost(32 * student_width * 4, mega),
    )(mine, *received)


def weight_kernel(rows, own, other, *refs):
    over_rows = (((0,), (0,)), ((), ()))
    refs[-1][...] = (
        lax.dot_general(rows[:half], own[...], over_rows, preferred_element_type=jnp.float32)
        + lax.dot_general(rows[half:], other[...], over_rows, preferred_element_type=jnp.float32)
    ).astype(jnp.bfloat16)


def grad_weight_part(rows, own, other, first, steps, before=None, tile=256):
    more = [] if before is None else [before]
    return pl.pallas_call(
        weight_kernel,
        grid=(steps,),
        in_specs=[pl.BlockSpec((tokens, tile), lambda j: (0, first + j)), whole(), whole()]
        + [pl.BlockSpec(memory_space=pl.ANY)] * len(more),
        out_specs=pl.BlockSpec((tile, vocab_local), lambda j: (first + j, 0)),
        out_shape=jax.ShapeDtypeStruct((student_width, vocab_local), jnp.bfloat16),
        input_output_aliases={3: 0} if more else {},
        compiler_params=pltpu.CompilerParams(vmem_limit_bytes=9 * mega),
        cost_estimate=cost(tokens * steps * tile * vocab_local, 2 * steps * tile * vocab_local),
    )(rows, own, other, *more)


def local(hidden_teacher, hidden_student, teacher_weight, student_weight, token_weight):
    main_order, apart_order, reduce_order, weight_here, first_core = setup(
        token_weight, teacher_weight
    )

    def shared_along(block, axes):
        return [block] + [send(block, axes, by) for by in offsets[1:]]

    def joined(blocks):
        return jnp.concatenate(blocks, axis=0)

    block = joined(shared_along(side_by_side(hidden_teacher, hidden_student), main_axes[0]))
    separate, main = block[:, :apart], block[:, apart:]
    main, separate = shared_along(main, main_axes[1]), shared_along(separate, apart_axes[1])
    main, *separate = lax.optimization_barrier((joined(main), *separate))
    separate = joined(separate)
    main = shared_along(main, main_axes[2])
    separate = shared_along(separate, apart_axes[2])
    teacher_own, teacher_other = teacher_logits(main_order, main, teacher_weight)
    teacher_other, *separate = lax.optimization_barrier((teacher_other, *separate))
    teacher_raw = (teacher_own, swap(teacher_other))
    cols = vocab_local // 2
    own, other, rows = student_logits(main_order, apart_order, main, separate, student_weight, cols)
    student_raw0 = (own, swap(other))
    own, other = student_rest(rows, student_weight, cols)
    student_raw1 = (own, swap(other))
    student_part0, teacher_part0, sums = statistics(teacher_raw, student_raw0, 0)
    student_part1, teacher_part1, sums = statistics(teacher_raw, student_raw1, 1, sums)
    for axes in reduce_axes:
        sums = sum(shared_along(sums, axes))
    gap, divergence = gap_of(
        sums, weight_here, (student_part0, teacher_part0, student_part1, teacher_part1)
    )
    gap_other = swap(gap)

    def sent_back(sends, axes):
        return [send(b, axes, -by) for b, by in zip(sends, offsets[1:])]

    gap_order, keep0, *sends = hidden_first(reduce_order, gap, gap_other, student_weight)
    received0 = sent_back(sends, reduce_axes[0])
    keep1, *sends = hidden_second(gap_order, student_weight)
    received1 = sent_back(sends, reduce_axes[0])
    divergence_other = swap(divergence)
    grad_weight = grad_weight_part(rows, gap, gap_other, 0, 4)
    keep0, grad_weight, divergence_other = lax.optimization_barrier(
        (keep0, grad_weight, divergence_other)
    )
    keep, *sends = first_sum(((keep0, *received0), (keep1, *received1)))
    received = sent_back(sends, reduce_axes[1])
    grad_weight = grad_weight_part(rows, gap, gap_other, 4, 3, grad_weight)
    keep, grad_weight = lax.optimization_barrier((keep, grad_weight))
    keep, *sends = second_sum(keep, received)
    received = sent_back(sends, reduce_axes[2])
    grad_hidden = (keep + sum(received)).astype(jnp.bfloat16)

    first_core = first_core > 0.5
    divergence = jnp.concatenate(
        [
            jnp.where(first_core, divergence, divergence_other),
            jnp.where(first_core, divergence_other, divergence),
        ]
    ).reshape(tokens)
    return (divergence, grad_hidden, grad_weight)


def solution(mesh):
    placed = (
        P(("batch", "vocab"), "mp"),
        P(("batch", "vocab"), "mp"),
        P("mp", ("batch", "vocab")),
        P("mp", ("batch", "vocab")),
        P(),
    )
    return jax.shard_map(
        local,
        mesh=mesh,
        in_specs=placed,
        out_specs=(P(), P(("batch", "vocab"), "mp"), P("mp", ("batch", "vocab"))),
        check_vma=False,
    )
```

```python
import functools

import jax
import jax.numpy as jnp
import numpy as np
from jax import lax
from jax.experimental import pallas as pl
from jax.experimental.pallas import tpu as pltpu
from jax.sharding import PartitionSpec as P

softcap_limit = 30.0
tokens, teacher_width, student_width, vocab_local = 512, 2304, 1792, 2048
width = teacher_width + student_width
half = tokens // 2
apart = 1536
everyone = ("mp", "batch", "vocab")
mega = 1024 * 1024

offsets = (0, 1, 3, 2)
main_axes = (("y", "z"), ("x", "x"), ("z", "y"))
apart_axes = (("y", "z"), ("z", "y"), ("x", "x"))
reduce_axes = (("z", "y"), ("x", "z"), ("y", "x"))


def place(index):
    core, z, x_lo, y, x_hi = np.unravel_index(index, (2, 4, 2, 4, 2))
    return {"core": int(core), "x": int(2 * x_hi + x_lo), "y": int(y), "z": int(z)}


def index_of(at):
    return int(
        np.ravel_multi_index(
            (at["core"], at["z"], at["x"] % 2, at["y"], at["x"] // 2), (2, 4, 2, 4, 2)
        )
    )


def moved(at, axis, by):
    return {**at, axis: (at[axis] + by) % 4}


def ring(axes, by):
    pairs = []
    for source in range(128):
        at = place(source)
        pairs.append((source, index_of(moved(at, axes[at["core"]], by))))
    return pairs


def send(block, axes, by):
    return lax.ppermute(block, everyone, ring(axes, by))


def swap(block):
    return lax.ppermute(block, "mp", [(0, 1), (1, 0)])


def side_by_side_kernel(teacher, student, out, held_teacher, held_student, arrived):
    copies = [
        pltpu.make_async_copy(teacher, held_teacher, arrived.at[0]),
        pltpu.make_async_copy(student, held_student, arrived.at[1]),
    ]
    for copy in copies:
        copy.start()
    for copy in copies:
        copy.wait()
    out[:, :apart] = held_student[:, :apart]
    out[:, apart : apart + teacher_width] = held_teacher[...]
    out[:, apart + teacher_width :] = held_student[:, apart:]


def side_by_side(teacher, student):
    return pl.pallas_call(
        side_by_side_kernel,
        in_specs=[pl.BlockSpec(memory_space=pl.ANY)] * 2,
        out_specs=whole(),
        out_shape=jax.ShapeDtypeStruct((teacher.shape[0], width), teacher.dtype),
        scratch_shapes=[
            pltpu.VMEM(teacher.shape, teacher.dtype),
            pltpu.VMEM(student.shape, student.dtype),
            pltpu.SemaphoreType.DMA((2,)),
        ],
        compiler_params=pltpu.CompilerParams(vmem_limit_bytes=mega),
        cost_estimate=cost(0, 4 * teacher.shape[0] * width),
    )(teacher, student)


def gathered(order, blocks, first, rows):
    step = 256
    for at in range(0, rows.shape[1], step):
        cols = slice(first + at, first + at + step)
        block = jnp.concatenate([x[:, cols] for x in blocks], axis=0)
        rows[:, at : at + step] = jnp.dot(
            order[...], block, preferred_element_type=jnp.float32
        ).astype(jnp.bfloat16)


def logits(rows, weight, first, own, other):
    step = 512
    for at in range(0, own.shape[1], step):
        raw = jnp.dot(
            rows[...], weight[:, first + at : first + at + step], preferred_element_type=jnp.float32
        )
        own[:, at : at + step], other[:, at : at + step] = raw[:half], raw[half:]


def placed(places, which, block):
    return pl.ds(pl.multiple_of(places[which, block], 8), 8)


def teacher_kernel(places, x0, x1, x2, x3, weight, own, other, rows, raw):
    for i, x in enumerate((x0, x1, x2, x3)):
        rows[128 * i : 128 * (i + 1)] = x[:, :teacher_width]
    step = raw.shape[2]
    for i, at in enumerate(range(0, vocab_local, step)):
        cols, held = slice(at, at + step), raw.at[i % 2]
        term = jnp.dot(rows[...], weight[:, cols], preferred_element_type=jnp.float32)
        for block in range(64):
            held[placed(places, 0, block)] = term[8 * block : 8 * (block + 1)]
        own[:, cols], other[:, cols] = held[:half], held[half:]


def student_kernel(main_order, apart_order, *refs):
    main, separate, (weight, own, other, rows) = refs[:4], refs[4:8], refs[8:]
    gathered(apart_order, separate, 0, rows.at[:, :apart])
    gathered(main_order, main, teacher_width, rows.at[:, apart:])
    logits(rows, weight, 0, own, other)


def student_rest_kernel(rows, weight, own, other):
    logits(rows, weight, vocab_local - own.shape[1], own, other)


def own_place(token, at, axes_of, core):
    block, row = token // 8, token % 8
    for stage, axes in enumerate(axes_of):
        digit = (block >> (2 * stage)) & 3
        offset = digit ^ (digit >> 1)
        for axis in at:
            taken = (axes[0] == axis) * (1 - core) + (axes[1] == axis) * core
            at[axis] = at[axis] - taken * offset
    x, y, z = (at[axis] & 3 for axis in "xyz")
    owner = z * 16 + (x & 1) * 8 + y * 2 + (x >> 1)
    return ((owner - 32 * core) & 63) * 8 + row


def setup_kernel(_, main_order, apart_order, places, first_core):
    core = lax.axis_index("mp")
    batch, vocab = lax.axis_index("batch"), lax.axis_index("vocab")
    at = {"x": (vocab % 2) * 2 + batch % 2, "y": vocab // 2, "z": batch // 2}
    token = lax.broadcasted_iota(jnp.int32, (1, tokens), 1)
    rows = lax.broadcasted_iota(jnp.int32, (tokens, tokens), 0)
    for order, axes_of in ((main_order, main_axes), (apart_order, apart_axes)):
        goal = own_place(token, dict(at), axes_of, core)
        order[...] = jnp.where(rows == goal, 1.0, 0.0).astype(jnp.bfloat16)
    block = lax.broadcasted_iota(jnp.int32, (1, 128), 1) % 64 * 8
    for i, axes_of in enumerate((main_axes, reduce_axes[::-1])):
        places[i : i + 1] = own_place(block, dict(at), axes_of, core)
    first_core[...] = jnp.full(first_core.shape, 1.0, jnp.float32) * (core == 0).astype(jnp.float32)


def setup(weight):
    order = jax.ShapeDtypeStruct((tokens, tokens), jnp.bfloat16)
    small = jax.ShapeDtypeStruct((2, 128), jnp.float32)
    return pl.pallas_call(
        setup_kernel,
        in_specs=[pl.BlockSpec(memory_space=pl.ANY)],
        out_specs=[whole()] * 4,
        out_shape=[order] * 2 + [jax.ShapeDtypeStruct((2, 128), jnp.int32), small],
        compiler_params=pltpu.CompilerParams(vmem_limit_bytes=4 * mega),
        cost_estimate=cost(0, 2 * mega),
    )(weight)


def cost(macs, moved, transcendentals=0):
    return pl.CostEstimate(flops=2 * macs, bytes_accessed=moved, transcendentals=transcendentals)


def whole():
    return pl.BlockSpec(memory_space=pltpu.VMEM)


def raw_shapes(cols):
    return [jax.ShapeDtypeStruct((half, cols), jnp.float32)] * 2


def scalars():
    return pl.BlockSpec(memory_space=pltpu.SMEM)


def teacher_logits(places, blocks, weight):
    return pl.pallas_call(
        teacher_kernel,
        in_specs=[scalars()] + [whole()] * 5,
        out_specs=[whole()] * 2,
        out_shape=raw_shapes(vocab_local),
        scratch_shapes=[
            pltpu.VMEM((tokens, teacher_width), jnp.bfloat16),
            pltpu.VMEM((2, tokens, 512), jnp.float32),
        ],
        compiler_params=pltpu.CompilerParams(vmem_limit_bytes=26 * mega),
        cost_estimate=cost(tokens * weight.size, 2 * weight.size),
    )(places, *blocks, weight)


def student_logits(main_order, apart_order, main, separate, weight, cols):
    return pl.pallas_call(
        student_kernel,
        in_specs=[whole()] * 11,
        out_specs=[whole()] * 3,
        out_shape=raw_shapes(cols) + [jax.ShapeDtypeStruct((tokens, student_width), jnp.bfloat16)],
        compiler_params=pltpu.CompilerParams(vmem_limit_bytes=20 * mega),
        cost_estimate=cost(tokens * student_width * cols, 2 * weight.size),
    )(main_order, apart_order, *main, *separate, weight)


def student_rest(rows, weight, cols):
    return pl.pallas_call(
        student_rest_kernel,
        in_specs=[whole()] * 2,
        out_specs=[whole()] * 2,
        out_shape=raw_shapes(cols),
        compiler_params=pltpu.CompilerParams(vmem_limit_bytes=16 * mega),
        cost_estimate=cost(tokens * student_width * cols, 2 * weight.size),
    )(rows, weight)


def lanes(values):
    total = values[:, :128]
    for at in range(128, values.shape[1], 128):
        total += values[:, at : at + 128]
    return total


def capped_exp(own, other):
    ratio = jnp.tanh((own[...] + other[...]) * (1.0 / softcap_limit))
    return ratio, jnp.exp(softcap_limit * ratio - softcap_limit)


def teacher_statistics_kernel(own, other, tanh, exp, total):
    @pl.when(pl.program_id(0) == 0)
    def _():
        total[...] = jnp.zeros_like(total)

    tanh[...], exp[...] = capped_exp(own, other)
    total[...] += lanes(exp[...])


def teacher_statistics(own, other, tile=256):
    block = pl.BlockSpec((half, tile), lambda j: (0, j))
    return pl.pallas_call(
        teacher_statistics_kernel,
        grid=(vocab_local // tile,),
        in_specs=[block] * 2,
        out_specs=[block] * 2 + [whole()],
        out_shape=raw_shapes(vocab_local) + [jax.ShapeDtypeStruct((half, 128), jnp.float32)],
        compiler_params=pltpu.CompilerParams(vmem_limit_bytes=7 * mega),
        cost_estimate=cost(4 * half * vocab_local, 16 * half * vocab_local, 2 * half * vocab_local),
    )(own, other)


def student_statistics_kernel(last, *refs):
    before, teacher_total = refs[:2] if last else (None, None)
    tanh, exp, own, other, student_part, teacher_part, out, sums = refs[2 if last else 0 :]

    @pl.when(pl.program_id(0) == 0)
    def _():
        sums[...] = before[...] if last else jnp.zeros_like(sums)

    student_tanh, student_exp = capped_exp(own, other)
    slope = 1.0 - student_tanh * student_tanh
    student_part[...] = student_exp * slope
    teacher_part[...] = exp[...] * slope
    sums[0] += lanes(student_exp)
    sums[1] += lanes(exp[...] * (softcap_limit * (tanh[...] - student_tanh)))

    @pl.when(pl.program_id(0) == pl.num_programs(0) - 1)
    def _():
        if last:
            rows = [
                jnp.sum(total[at : at + 128].T, axis=0, keepdims=True)
                for total in (teacher_total, sums.at[0], sums.at[1])
                for at in (0, 128)
            ]
            out[...] = jnp.concatenate(rows + [jnp.zeros((2, 128), jnp.float32)], axis=0)
        else:
            out[...] = sums[...]


def student_statistics(teacher, student, first, before=None, tile=256):
    cols = student[0].shape[1]
    last = before is not None
    from_teacher = pl.BlockSpec((half, tile), lambda j: (0, first // tile + j))
    part = pl.BlockSpec((half, tile), lambda j: (0, j))
    sums = (2, half, 128)
    tanh, exp, teacher_total = teacher
    return pl.pallas_call(
        functools.partial(student_statistics_kernel, last),
        grid=(cols // tile,),
        in_specs=[whole()] * (2 * last) + [from_teacher] * 2 + [part] * 2,
        out_specs=[part, part, whole()],
        out_shape=raw_shapes(cols) + [jax.ShapeDtypeStruct((8, 128) if last else sums, jnp.float32)],
        scratch_shapes=[pltpu.VMEM(sums, jnp.float32)],
        compiler_params=pltpu.CompilerParams(vmem_limit_bytes=7 * mega),
        cost_estimate=cost(8 * half * cols, 24 * half * cols, 2 * half * cols),
    )(*([before, teacher_total] if last else []), tanh, exp, *student)


def gap_kernel(total, token_weight, student0, teacher0, student1, teacher1, gap, divergence):
    teacher_total, student_total, cross = total[0:2], total[2:4], total[4:6]
    divergence[...] = cross / teacher_total - jnp.log(teacher_total) + jnp.log(student_total)
    mine = token_weight[pl.ds(lax.axis_index("mp") * 2, 2), :]
    rows = [mine / student_total, mine / teacher_total, total[0:4]]
    scales = jnp.concatenate(rows, axis=0).T
    cols = student0.shape[1]
    for i in range(2):
        at = slice(128 * i, 128 * (i + 1))
        student_scale, teacher_scale = scales[:, i : i + 1], scales[:, 2 + i : 3 + i]
        for first, student, teacher in ((0, student0, teacher0), (cols, student1, teacher1)):
            gap[at, first : first + student.shape[1]] = (
                student[at] * student_scale - teacher[at] * teacher_scale
            ).astype(jnp.bfloat16)


def gap_of(total, token_weight, parts):
    return pl.pallas_call(
        gap_kernel,
        in_specs=[whole()] * 6,
        out_specs=[whole(), whole()],
        out_shape=[
            jax.ShapeDtypeStruct((half, vocab_local), jnp.bfloat16),
            jax.ShapeDtypeStruct((2, 128), jnp.float32),
        ],
        compiler_params=pltpu.CompilerParams(vmem_limit_bytes=4 * mega),
        cost_estimate=cost(2 * half * vocab_local, 10 * half * vocab_local),
    )(total, token_weight, *parts)


def hidden_term(gap, weight):
    return lax.dot_general(
        gap[...], weight, (((1,), (1,)), ((), ())), preferred_element_type=jnp.float32
    )


def column_tiles(tile=256):
    return [slice(at, at + tile) for at in range(0, student_width, tile)]


def hidden_own_kernel(gap, weight, out):
    for cols in column_tiles():
        out[:, cols] = hidden_term(gap, weight[cols])


def hidden_own(gap, weight):
    return pl.pallas_call(
        hidden_own_kernel,
        in_specs=[whole()] * 2,
        out_specs=whole(),
        out_shape=jax.ShapeDtypeStruct((half, student_width), jnp.float32),
        compiler_params=pltpu.CompilerParams(vmem_limit_bytes=14 * mega),
        cost_estimate=cost(half * weight.size, 2 * weight.size),
    )(gap, weight)


def hidden_all_kernel(places, own, gap, weight, keep, send1, send2, send3, term):
    for cols in column_tiles():
        term[:half, cols] = own[:, cols]
        term[half:, cols] = hidden_term(gap, weight[cols])
        for pair in range(32):
            both = [term[placed(places, 1, 2 * pair + i), cols] for i in range(2)]
            both = jnp.concatenate(both, axis=0)
            out = (keep, send1, send2, send3)[pair // 8]
            at = 16 * (pair % 8)
            out[at : at + 16, cols] = both.astype(out.dtype)


def hidden_all(places, own, gap, weight):
    return pl.pallas_call(
        hidden_all_kernel,
        in_specs=[scalars()] + [whole()] * 3,
        out_specs=[whole()] * 4,
        out_shape=[jax.ShapeDtypeStruct((128, student_width), jnp.float32)]
        + [jax.ShapeDtypeStruct((128, student_width), jnp.bfloat16)] * 3,
        scratch_shapes=[pltpu.VMEM((tokens, student_width), jnp.float32)],
        compiler_params=pltpu.CompilerParams(vmem_limit_bytes=22 * mega),
        cost_estimate=cost(half * weight.size, 2 * weight.size),
    )(places, own, gap, weight)


def total_of(keep, received, at, size):
    rows = pl.ds(at, size)
    return keep[rows] + sum(r[rows].astype(jnp.float32) for r in received)


def first_sum_kernel(mine, *refs):
    received, (keep, *sends) = refs[:3], refs[3:]
    keep[...] = total_of(mine, received, 0, 32)
    for j, send in enumerate(sends):
        send[...] = total_of(mine, received, 32 * (j + 1), 32).astype(send.dtype)


def first_sum(mine, received):
    shape = (32, student_width)
    return pl.pallas_call(
        first_sum_kernel,
        in_specs=[whole()] * 4,
        out_specs=[whole()] * 4,
        out_shape=[jax.ShapeDtypeStruct(shape, jnp.float32)]
        + [jax.ShapeDtypeStruct(shape, jnp.bfloat16)] * 3,
        compiler_params=pltpu.CompilerParams(vmem_limit_bytes=6 * mega),
        cost_estimate=cost(128 * student_width * 4, 2 * mega),
    )(mine, *received)


def second_sum_kernel(mine, *refs):
    received, (keep, *sends) = refs[:3], refs[3:]
    total = mine[...] + sum(r[...].astype(jnp.float32) for r in received)
    keep[...] = total[:8]
    for j, send in enumerate(sends):
        send[...] = total[8 * (j + 1) : 8 * (j + 2)]


def second_sum(mine, received):
    return pl.pallas_call(
        second_sum_kernel,
        in_specs=[whole()] * 4,
        out_specs=[whole()] * 4,
        out_shape=[jax.ShapeDtypeStruct((8, student_width), jnp.float32)] * 4,
        compiler_params=pltpu.CompilerParams(vmem_limit_bytes=3 * mega),
        cost_estimate=cost(32 * student_width * 4, mega),
    )(mine, *received)


def grad_weight_kernel(rows, own, other, out):
    over_rows = (((0,), (0,)), ((), ()))
    out[...] = (
        lax.dot_general(rows[:half], own[...], over_rows, preferred_element_type=jnp.float32)
        + lax.dot_general(rows[half:], other[...], over_rows, preferred_element_type=jnp.float32)
    ).astype(jnp.bfloat16)


def grad_weight_of(rows, own, other, tile=256):
    return pl.pallas_call(
        grad_weight_kernel,
        grid=(student_width // tile,),
        in_specs=[pl.BlockSpec((tokens, tile), lambda j: (0, j)), whole(), whole()],
        out_specs=pl.BlockSpec((tile, vocab_local), lambda j: (j, 0)),
        out_shape=jax.ShapeDtypeStruct((student_width, vocab_local), jnp.bfloat16),
        compiler_params=pltpu.CompilerParams(vmem_limit_bytes=9 * mega),
        cost_estimate=cost(tokens * student_width * vocab_local, 2 * student_width * vocab_local),
    )(rows, own, other)


def local(hidden_teacher, hidden_student, teacher_weight, student_weight, token_weight):
    main_order, apart_order, places, first_core = setup(teacher_weight)

    def shared_along(block, axes):
        return [block] + [send(block, axes, by) for by in offsets[1:]]

    def joined(blocks):
        return jnp.concatenate(blocks, axis=0)

    block = joined(shared_along(side_by_side(hidden_teacher, hidden_student), main_axes[0]))
    separate, main = block[:, :apart], block[:, apart:]
    main, separate = shared_along(main, main_axes[1]), shared_along(separate, apart_axes[1])
    main = joined(main)
    _, *separate = lax.optimization_barrier((main, *separate))
    separate = joined(separate)
    main = shared_along(main, main_axes[2])
    separate = shared_along(separate, apart_axes[2])
    teacher_own, teacher_other = teacher_logits(places, main, teacher_weight)
    teacher_other, *separate = lax.optimization_barrier((teacher_other, *separate))
    teacher_other = swap(teacher_other)
    cols = 1536
    own0, other0, rows = student_logits(
        main_order, apart_order, main, separate, student_weight, cols
    )
    other0 = swap(other0)
    own1, other1 = student_rest(rows, student_weight, vocab_local - cols)
    teacher_own, other1 = lax.optimization_barrier((teacher_own, other1))
    other1 = swap(other1)
    teacher = teacher_statistics(teacher_own, teacher_other)
    student_part0, teacher_part0, sums = student_statistics(teacher, (own0, other0), 0)
    student_part1, teacher_part1, sums = student_statistics(teacher, (own1, other1), cols, sums)
    for axes in reduce_axes:
        sums = sum(shared_along(sums, axes))
    gap, divergence = gap_of(
        sums, token_weight.reshape(4, 128), (student_part0, teacher_part0, student_part1, teacher_part1)
    )
    gap_other, divergence_other = lax.optimization_barrier((swap(gap), swap(divergence)))

    def sent_back(sends, axes):
        return [send(b, axes, -by) for b, by in zip(sends, offsets[1:])]

    hidden = hidden_own(gap, student_weight)
    gap_other, hidden = lax.optimization_barrier((gap_other, hidden))
    keep, *sends = hidden_all(places, hidden, gap_other, student_weight)
    received = sent_back(sends, reduce_axes[0])
    grad_weight = grad_weight_of(rows, gap, gap_other)
    keep, grad_weight = lax.optimization_barrier((keep, grad_weight))
    keep, *sends = first_sum(keep, received)
    received = sent_back(sends, reduce_axes[1])
    keep, *sends = second_sum(keep, received)
    received = sent_back(sends, reduce_axes[2])
    grad_hidden = (keep + sum(received)).astype(jnp.bfloat16)

    first_core = first_core > 0.5
    divergence = jnp.concatenate(
        [
            jnp.where(first_core, divergence, divergence_other),
            jnp.where(first_core, divergence_other, divergence),
        ]
    ).reshape(tokens)
    return (divergence, grad_hidden, grad_weight)


def solution(mesh):
    placed = (
        P(("batch", "vocab"), "mp"),
        P(("batch", "vocab"), "mp"),
        P("mp", ("batch", "vocab")),
        P("mp", ("batch", "vocab")),
        P(),
    )
    return jax.shard_map(
        local,
        mesh=mesh,
        in_specs=placed,
        out_specs=(P(), P(("batch", "vocab"), "mp"), P("mp", ("batch", "vocab"))),
        check_vma=False,
    )
```

```python
import functools

import jax
import jax.numpy as jnp
import numpy as np
from jax import lax
from jax.experimental import pallas as pl
from jax.experimental.pallas import tpu as pltpu
from jax.sharding import PartitionSpec as P

softcap_limit = 30.0
tokens, teacher_width, student_width, vocab_local = 512, 2304, 1792, 2048
width = teacher_width + student_width
half = tokens // 2
apart = 1664
everyone = ("mp", "batch", "vocab")
mega = 1024 * 1024

offsets = (0, 1, 3, 2)
main_axes = (("y", "z"), ("x", "x"), ("z", "y"))
apart_axes = (("y", "z"), ("z", "y"), ("x", "x"))
reduce_axes = (("z", "y"), ("x", "z"), ("y", "x"))


def place(index):
    core, z, x_lo, y, x_hi = np.unravel_index(index, (2, 4, 2, 4, 2))
    return {"core": int(core), "x": int(2 * x_hi + x_lo), "y": int(y), "z": int(z)}


def index_of(at):
    return int(
        np.ravel_multi_index(
            (at["core"], at["z"], at["x"] % 2, at["y"], at["x"] // 2), (2, 4, 2, 4, 2)
        )
    )


def moved(at, axis, by):
    return {**at, axis: (at[axis] + by) % 4}


def ring(axes, by):
    pairs = []
    for source in range(128):
        at = place(source)
        pairs.append((source, index_of(moved(at, axes[at["core"]], by))))
    return pairs


def planes():
    groups = {}
    for index in range(128):
        at = place(index)
        groups.setdefault((at["core"], at[reduce_axes[0][at["core"]]]), []).append(index)
    return list(groups.values())


def send(block, axes, by):
    return lax.ppermute(block, everyone, ring(axes, by))


def swap(block):
    return lax.ppermute(block, "mp", [(0, 1), (1, 0)])


def side_by_side_kernel(teacher, student, out, held_teacher, held_student, arrived):
    copies = [
        pltpu.make_async_copy(teacher, held_teacher, arrived.at[0]),
        pltpu.make_async_copy(student, held_student, arrived.at[1]),
    ]
    for copy in copies:
        copy.start()
    for copy in copies:
        copy.wait()
    out[:, :apart] = held_student[:, :apart]
    out[:, apart : apart + teacher_width] = held_teacher[...]
    out[:, apart + teacher_width :] = held_student[:, apart:]


def side_by_side(teacher, student):
    return pl.pallas_call(
        side_by_side_kernel,
        in_specs=[pl.BlockSpec(memory_space=pl.ANY)] * 2,
        out_specs=whole(),
        out_shape=jax.ShapeDtypeStruct((teacher.shape[0], width), teacher.dtype),
        scratch_shapes=[
            pltpu.VMEM(teacher.shape, teacher.dtype),
            pltpu.VMEM(student.shape, student.dtype),
            pltpu.SemaphoreType.DMA((2,)),
        ],
        compiler_params=pltpu.CompilerParams(vmem_limit_bytes=mega),
        cost_estimate=cost(0, 4 * teacher.shape[0] * width),
    )(teacher, student)


def gathered(order, blocks, first, rows):
    step = 512
    for at in range(0, rows.shape[1], step):
        end = min(at + step, rows.shape[1])
        block = jnp.concatenate([x[:, first + at : first + end] for x in blocks], axis=0)
        rows[:, at:end] = jnp.dot(
            order[...], block, preferred_element_type=jnp.float32
        ).astype(jnp.bfloat16)


def logits(rows, weight, first, own, other):
    step = 512
    for at in range(0, own.shape[1], step):
        raw = jnp.dot(
            rows[...], weight[:, first + at : first + at + step], preferred_element_type=jnp.float32
        )
        own[:, at : at + step], other[:, at : at + step] = raw[:half], raw[half:]


def placed(places, which, block):
    return pl.ds(pl.multiple_of(places[which, block], 8), 8)


def teacher_kernel(places, x0, x1, x2, x3, weight, own, other, rows, raw):
    for i, x in enumerate((x0, x1, x2, x3)):
        rows[128 * i : 128 * (i + 1)] = x[:, :teacher_width]
    step = raw.shape[2]
    for i, at in enumerate(range(0, vocab_local, step)):
        cols, held = slice(at, at + step), raw.at[i % 2]
        term = jnp.dot(rows[...], weight[:, cols], preferred_element_type=jnp.float32)
        for block in range(64):
            held[placed(places, 0, block)] = term[8 * block : 8 * (block + 1)]
        own[:, cols], other[:, cols] = held[:half], held[half:]


def student_kernel(main_order, apart_order, *refs):
    main, separate, (weight, own, other, rows) = refs[:4], refs[4:8], refs[8:]
    gathered(apart_order, separate, 0, rows.at[:, :apart])
    gathered(main_order, main, teacher_width, rows.at[:, apart:])
    logits(rows, weight, 0, own, other)


def student_rest_kernel(rows, weight, own, other):
    logits(rows, weight, vocab_local - own.shape[1], own, other)


def own_place(token, at, axes_of, core):
    block, row = token // 8, token % 8
    for stage, axes in enumerate(axes_of):
        digit = (block >> (2 * stage)) & 3
        offset = digit ^ (digit >> 1)
        for axis in at:
            taken = (axes[0] == axis) * (1 - core) + (axes[1] == axis) * core
            at[axis] = at[axis] - taken * offset
    x, y, z = (at[axis] & 3 for axis in "xyz")
    owner = z * 16 + (x & 1) * 8 + y * 2 + (x >> 1)
    return ((owner - 32 * core) & 63) * 8 + row


def reduce_place(row, at, core):
    block = row // 8
    digit, member = block >> 4, block & 15
    offset = digit ^ (digit >> 1)
    z = (1 - core) * ((at["z"] - offset) & 3) + core * (member >> 2)
    y = (1 - core) * ((member >> 1) & 3) + core * ((at["y"] - offset) & 3)
    x_lo = (1 - core) * (member >> 3) + core * ((member >> 1) & 1)
    owner = z * 16 + x_lo * 8 + y * 2 + (member & 1)
    return ((owner - 32 * core) & 63) * 8 + row % 8


def setup_kernel(_, main_order, apart_order, places, first_core):
    core = lax.axis_index("mp")
    batch, vocab = lax.axis_index("batch"), lax.axis_index("vocab")
    at = {"x": (vocab % 2) * 2 + batch % 2, "y": vocab // 2, "z": batch // 2}
    token = lax.broadcasted_iota(jnp.int32, (1, tokens), 1)
    rows = lax.broadcasted_iota(jnp.int32, (tokens, tokens), 0)
    for order, axes_of in ((main_order, main_axes), (apart_order, apart_axes)):
        goal = own_place(token, dict(at), axes_of, core)
        order[...] = jnp.where(rows == goal, 1.0, 0.0).astype(jnp.bfloat16)
    block = lax.broadcasted_iota(jnp.int32, (1, 128), 1) % 64 * 8
    places[0:1] = own_place(block, dict(at), main_axes, core)
    places[1:2] = reduce_place(block, at, core)
    first_core[...] = jnp.full(first_core.shape, 1.0, jnp.float32) * (core == 0).astype(jnp.float32)


def setup(weight):
    order = jax.ShapeDtypeStruct((tokens, tokens), jnp.bfloat16)
    small = jax.ShapeDtypeStruct((2, 128), jnp.float32)
    return pl.pallas_call(
        setup_kernel,
        in_specs=[pl.BlockSpec(memory_space=pl.ANY)],
        out_specs=[whole()] * 4,
        out_shape=[order] * 2 + [jax.ShapeDtypeStruct((2, 128), jnp.int32), small],
        compiler_params=pltpu.CompilerParams(vmem_limit_bytes=4 * mega),
        cost_estimate=cost(0, 2 * mega),
    )(weight)


def cost(macs, moved, transcendentals=0):
    return pl.CostEstimate(flops=2 * macs, bytes_accessed=moved, transcendentals=transcendentals)


def whole():
    return pl.BlockSpec(memory_space=pltpu.VMEM)


def raw_shapes(cols):
    return [jax.ShapeDtypeStruct((half, cols), jnp.float32)] * 2


def scalars():
    return pl.BlockSpec(memory_space=pltpu.SMEM)


def teacher_logits(places, blocks, weight):
    return pl.pallas_call(
        teacher_kernel,
        in_specs=[scalars()] + [whole()] * 5,
        out_specs=[whole()] * 2,
        out_shape=raw_shapes(vocab_local),
        scratch_shapes=[
            pltpu.VMEM((tokens, teacher_width), jnp.bfloat16),
            pltpu.VMEM((2, tokens, 512), jnp.float32),
        ],
        compiler_params=pltpu.CompilerParams(vmem_limit_bytes=26 * mega),
        cost_estimate=cost(tokens * weight.size, 2 * weight.size),
    )(places, *blocks, weight)


def student_logits(main_order, apart_order, main, separate, weight, cols):
    return pl.pallas_call(
        student_kernel,
        in_specs=[whole()] * 11,
        out_specs=[whole()] * 3,
        out_shape=raw_shapes(cols) + [jax.ShapeDtypeStruct((tokens, student_width), jnp.bfloat16)],
        compiler_params=pltpu.CompilerParams(vmem_limit_bytes=20 * mega),
        cost_estimate=cost(tokens * student_width * cols, 2 * weight.size),
    )(main_order, apart_order, *main, *separate, weight)


def student_rest(rows, weight, cols):
    return pl.pallas_call(
        student_rest_kernel,
        in_specs=[whole()] * 2,
        out_specs=[whole()] * 2,
        out_shape=raw_shapes(cols),
        compiler_params=pltpu.CompilerParams(vmem_limit_bytes=16 * mega),
        cost_estimate=cost(tokens * student_width * cols, 2 * weight.size),
    )(rows, weight)


def lanes(values):
    total = values[:, :128]
    for at in range(128, values.shape[1], 128):
        total += values[:, at : at + 128]
    return total


def capped_exp(own, other):
    ratio = jnp.tanh((own[...] + other[...]) * (1.0 / softcap_limit))
    return ratio, jnp.exp(softcap_limit * ratio - softcap_limit)


def teacher_statistics_kernel(own, other, tanh, exp, total):
    @pl.when(pl.program_id(0) == 0)
    def _():
        total[...] = jnp.zeros_like(total)

    tanh[...], exp[...] = capped_exp(own, other)
    total[...] += lanes(exp[...])


def teacher_statistics(own, other, tile=256):
    block = pl.BlockSpec((half, tile), lambda j: (0, j))
    return pl.pallas_call(
        teacher_statistics_kernel,
        grid=(vocab_local // tile,),
        in_specs=[block] * 2,
        out_specs=[block] * 2 + [whole()],
        out_shape=raw_shapes(vocab_local) + [jax.ShapeDtypeStruct((half, 128), jnp.float32)],
        compiler_params=pltpu.CompilerParams(vmem_limit_bytes=7 * mega),
        cost_estimate=cost(4 * half * vocab_local, 16 * half * vocab_local, 2 * half * vocab_local),
    )(own, other)


def student_statistics_kernel(last, *refs):
    before, teacher_total = refs[:2] if last else (None, None)
    tanh, exp, own, other, student_part, teacher_part, out, sums = refs[2 if last else 0 :]

    @pl.when(pl.program_id(0) == 0)
    def _():
        sums[...] = before[...] if last else jnp.zeros_like(sums)

    student_tanh, student_exp = capped_exp(own, other)
    slope = 1.0 - student_tanh * student_tanh
    student_part[...] = student_exp * slope
    teacher_part[...] = exp[...] * slope
    sums[0] += lanes(student_exp)
    sums[1] += lanes(exp[...] * (softcap_limit * (tanh[...] - student_tanh)))

    @pl.when(pl.program_id(0) == pl.num_programs(0) - 1)
    def _():
        if last:
            rows = [
                jnp.sum(total[at : at + 128].T, axis=0, keepdims=True)
                for total in (teacher_total, sums.at[0], sums.at[1])
                for at in (0, 128)
            ]
            out[...] = jnp.concatenate(rows + [jnp.zeros((2, 128), jnp.float32)], axis=0)
        else:
            out[...] = sums[...]


def student_statistics(teacher, student, first, before=None, tile=256):
    cols = student[0].shape[1]
    last = before is not None
    from_teacher = pl.BlockSpec((half, tile), lambda j: (0, first // tile + j))
    part = pl.BlockSpec((half, tile), lambda j: (0, j))
    sums = (2, half, 128)
    tanh, exp, teacher_total = teacher
    return pl.pallas_call(
        functools.partial(student_statistics_kernel, last),
        grid=(cols // tile,),
        in_specs=[whole()] * (2 * last) + [from_teacher] * 2 + [part] * 2,
        out_specs=[part, part, whole()],
        out_shape=raw_shapes(cols) + [jax.ShapeDtypeStruct((8, 128) if last else sums, jnp.float32)],
        scratch_shapes=[pltpu.VMEM(sums, jnp.float32)],
        compiler_params=pltpu.CompilerParams(vmem_limit_bytes=7 * mega),
        cost_estimate=cost(8 * half * cols, 24 * half * cols, 2 * half * cols),
    )(*([before, teacher_total] if last else []), tanh, exp, *student)


def gap_kernel(total, token_weight, student0, teacher0, student1, teacher1, gap, divergence):
    teacher_total, student_total, cross = total[0:2], total[2:4], total[4:6]
    divergence[...] = cross / teacher_total - jnp.log(teacher_total) + jnp.log(student_total)
    mine = token_weight[pl.ds(lax.axis_index("mp") * 2, 2), :]
    rows = [mine / student_total, mine / teacher_total, total[0:4]]
    scales = jnp.concatenate(rows, axis=0).T
    cols = student0.shape[1]
    for i in range(2):
        at = slice(128 * i, 128 * (i + 1))
        student_scale, teacher_scale = scales[:, i : i + 1], scales[:, 2 + i : 3 + i]
        for first, student, teacher in ((0, student0, teacher0), (cols, student1, teacher1)):
            gap[at, first : first + student.shape[1]] = (
                student[at] * student_scale - teacher[at] * teacher_scale
            ).astype(jnp.bfloat16)


def gap_of(total, token_weight, parts):
    return pl.pallas_call(
        gap_kernel,
        in_specs=[whole()] * 6,
        out_specs=[whole(), whole()],
        out_shape=[
            jax.ShapeDtypeStruct((half, vocab_local), jnp.bfloat16),
            jax.ShapeDtypeStruct((2, 128), jnp.float32),
        ],
        compiler_params=pltpu.CompilerParams(vmem_limit_bytes=4 * mega),
        cost_estimate=cost(2 * half * vocab_local, 10 * half * vocab_local),
    )(total, token_weight, *parts)


def hidden_term(gap, weight):
    return lax.dot_general(
        gap[...], weight, (((1,), (1,)), ((), ())), preferred_element_type=jnp.float32
    )


def column_tiles(tile=256):
    return [slice(at, at + tile) for at in range(0, student_width, tile)]


def hidden_own_kernel(gap, weight, out):
    for cols in column_tiles():
        out[:, cols] = hidden_term(gap, weight[cols])


def hidden_own(gap, weight):
    return pl.pallas_call(
        hidden_own_kernel,
        in_specs=[whole()] * 2,
        out_specs=whole(),
        out_shape=jax.ShapeDtypeStruct((half, student_width), jnp.float32),
        compiler_params=pltpu.CompilerParams(vmem_limit_bytes=14 * mega),
        cost_estimate=cost(half * weight.size, 2 * weight.size),
    )(gap, weight)


def hidden_all_kernel(places, own, gap, weight, keep, send1, send2, send3, term):
    for cols in column_tiles():
        term[:half, cols] = own[:, cols]
        term[half:, cols] = hidden_term(gap, weight[cols])
        for pair in range(32):
            both = [term[placed(places, 1, 2 * pair + i), cols] for i in range(2)]
            both = jnp.concatenate(both, axis=0)
            out = (keep, send1, send2, send3)[pair // 8]
            at = 16 * (pair % 8)
            out[at : at + 16, cols] = both.astype(out.dtype)


def hidden_all(places, own, gap, weight):
    return pl.pallas_call(
        hidden_all_kernel,
        in_specs=[scalars()] + [whole()] * 3,
        out_specs=[whole()] * 4,
        out_shape=[jax.ShapeDtypeStruct((128, student_width), jnp.float32)]
        + [jax.ShapeDtypeStruct((128, student_width), jnp.bfloat16)] * 3,
        scratch_shapes=[pltpu.VMEM((tokens, student_width), jnp.float32)],
        compiler_params=pltpu.CompilerParams(vmem_limit_bytes=22 * mega),
        cost_estimate=cost(half * weight.size, 2 * weight.size),
    )(places, own, gap, weight)


def first_sum_kernel(mine, *refs):
    received, out = refs[:3], refs[3]
    total = mine[...] + sum(r[...].astype(jnp.float32) for r in received)
    out[...] = total.astype(out.dtype)


def first_sum(mine, received):
    return pl.pallas_call(
        first_sum_kernel,
        in_specs=[whole()] * 4,
        out_specs=whole(),
        out_shape=jax.ShapeDtypeStruct(mine.shape, jnp.bfloat16),
        compiler_params=pltpu.CompilerParams(vmem_limit_bytes=6 * mega),
        cost_estimate=cost(128 * student_width * 4, 2 * mega),
    )(mine, *received)


def last_sum_kernel(received, out):
    total = received[0].astype(jnp.float32)
    for i in range(1, received.shape[0]):
        total += received[i].astype(jnp.float32)
    out[...] = total.astype(out.dtype)


def last_sum(received):
    return pl.pallas_call(
        last_sum_kernel,
        in_specs=[whole()],
        out_specs=whole(),
        out_shape=jax.ShapeDtypeStruct(received.shape[1:], received.dtype),
        compiler_params=pltpu.CompilerParams(vmem_limit_bytes=3 * mega),
        cost_estimate=cost(received.size, 2 * received.size),
    )(received)


def grad_weight_kernel(rows, own, other, out):
    over_rows = (((0,), (0,)), ((), ()))
    out[...] = (
        lax.dot_general(rows[:half], own[...], over_rows, preferred_element_type=jnp.float32)
        + lax.dot_general(rows[half:], other[...], over_rows, preferred_element_type=jnp.float32)
    ).astype(jnp.bfloat16)


def grad_weight_of(rows, own, other, tile=256):
    return pl.pallas_call(
        grad_weight_kernel,
        grid=(student_width // tile,),
        in_specs=[pl.BlockSpec((tokens, tile), lambda j: (0, j)), whole(), whole()],
        out_specs=pl.BlockSpec((tile, vocab_local), lambda j: (j, 0)),
        out_shape=jax.ShapeDtypeStruct((student_width, vocab_local), jnp.bfloat16),
        compiler_params=pltpu.CompilerParams(vmem_limit_bytes=9 * mega),
        cost_estimate=cost(tokens * student_width * vocab_local, 2 * student_width * vocab_local),
    )(rows, own, other)


def local(hidden_teacher, hidden_student, teacher_weight, student_weight, token_weight):
    main_order, apart_order, places, first_core = setup(teacher_weight)

    def shared_along(block, axes):
        return [block] + [send(block, axes, by) for by in offsets[1:]]

    def joined(blocks):
        return jnp.concatenate(blocks, axis=0)

    block = joined(shared_along(side_by_side(hidden_teacher, hidden_student), main_axes[0]))
    block, places = lax.optimization_barrier((block, places))
    separate, main = block[:, :apart], block[:, apart:]
    main, separate = shared_along(main, main_axes[1]), shared_along(separate, apart_axes[1])
    main = joined(main)
    _, *separate = lax.optimization_barrier((main, *separate))
    separate = joined(separate)
    main = shared_along(main, main_axes[2])
    separate = shared_along(separate, apart_axes[2])
    teacher_own, teacher_other = teacher_logits(places, main, teacher_weight)
    teacher_other, *separate = lax.optimization_barrier((teacher_other, *separate))
    teacher_other = swap(teacher_other)
    cols = 1536
    own0, other0, rows = student_logits(
        main_order, apart_order, main, separate, student_weight, cols
    )
    other0 = swap(other0)
    own1, other1 = student_rest(rows, student_weight, vocab_local - cols)
    teacher_own, other1 = lax.optimization_barrier((teacher_own, other1))
    other1 = swap(other1)
    teacher = teacher_statistics(teacher_own, teacher_other)
    student_part0, teacher_part0, sums = student_statistics(teacher, (own0, other0), 0)
    student_part1, teacher_part1, sums = student_statistics(teacher, (own1, other1), cols, sums)
    for axes in reduce_axes:
        sums = sum(shared_along(sums, axes))
    gap, divergence = gap_of(
        sums, token_weight.reshape(4, 128), (student_part0, teacher_part0, student_part1, teacher_part1)
    )
    gap_other, divergence_other = lax.optimization_barrier((swap(gap), swap(divergence)))

    def sent_back(sends, axes):
        far = send(sends[2], axes, -offsets[3])
        return [send(b, axes, -by) for b, by in zip(sends[:2], offsets[1:3])] + [far]

    hidden = hidden_own(gap, student_weight)
    gap_other, hidden = lax.optimization_barrier((gap_other, hidden))
    keep, *sends = hidden_all(places, hidden, gap_other, student_weight)
    received = sent_back(sends, reduce_axes[0])
    grad_weight = grad_weight_of(rows, gap, gap_other)
    keep, grad_weight = lax.optimization_barrier((keep, grad_weight))
    total = first_sum(keep, received).reshape(16, 8, student_width)
    total = lax.all_to_all(total, everyone, 0, 0, axis_index_groups=planes())
    grad_hidden = last_sum(total)

    first_core = first_core > 0.5
    divergence = jnp.concatenate(
        [
            jnp.where(first_core, divergence, divergence_other),
            jnp.where(first_core, divergence_other, divergence),
        ]
    ).reshape(tokens)
    return (divergence, grad_hidden, grad_weight)


def solution(mesh):
    placed = (
        P(("batch", "vocab"), "mp"),
        P(("batch", "vocab"), "mp"),
        P("mp", ("batch", "vocab")),
        P("mp", ("batch", "vocab")),
        P(),
    )
    return jax.shard_map(
        local,
        mesh=mesh,
        in_specs=placed,
        out_specs=(P(), P(("batch", "vocab"), "mp"), P("mp", ("batch", "vocab"))),
        check_vma=False,
    )
```

```python
import functools

import jax
import jax.numpy as jnp
import numpy as np
from jax import lax
from jax.experimental import pallas as pl
from jax.experimental.pallas import tpu as pltpu
from jax.sharding import PartitionSpec as P

softcap_limit = 30.0
tokens, teacher_width, student_width, vocab_local = 512, 2304, 1792, 2048
width = teacher_width + student_width
half = tokens // 2
apart = 1536
everyone = ("mp", "batch", "vocab")
mega = 1024 * 1024

offsets = (0, 1, 3, 2)
main_axes = (("y", "z"), ("x", "x"), ("z", "y"))
apart_axes = (("y", "z"), ("z", "y"), ("x", "x"))
reduce_axes = (("z", "y"), ("x", "z"), ("y", "x"))


def place(index):
    core, z, x_lo, y, x_hi = np.unravel_index(index, (2, 4, 2, 4, 2))
    return {"core": int(core), "x": int(2 * x_hi + x_lo), "y": int(y), "z": int(z)}


def index_of(at):
    return int(
        np.ravel_multi_index(
            (at["core"], at["z"], at["x"] % 2, at["y"], at["x"] // 2), (2, 4, 2, 4, 2)
        )
    )


def moved(at, axis, by):
    return {**at, axis: (at[axis] + by) % 4}


def ring(axes, by):
    pairs = []
    for source in range(128):
        at = place(source)
        pairs.append((source, index_of(moved(at, axes[at["core"]], by))))
    return pairs


def planes():
    groups = {}
    for index in range(128):
        at = place(index)
        groups.setdefault((at["core"], at[reduce_axes[0][at["core"]]]), []).append(index)
    return list(groups.values())


def send(block, axes, by):
    return lax.ppermute(block, everyone, ring(axes, by))


def swap(block):
    return lax.ppermute(block, "mp", [(0, 1), (1, 0)])


def side_by_side_kernel(teacher, student, out, held_teacher, held_student, arrived):
    copies = [
        pltpu.make_async_copy(teacher, held_teacher, arrived.at[0]),
        pltpu.make_async_copy(student, held_student, arrived.at[1]),
    ]
    for copy in copies:
        copy.start()
    for copy in copies:
        copy.wait()
    out[:, :apart] = held_student[:, :apart]
    out[:, apart : apart + teacher_width] = held_teacher[...]
    out[:, apart + teacher_width :] = held_student[:, apart:]


def side_by_side(teacher, student):
    return pl.pallas_call(
        side_by_side_kernel,
        in_specs=[pl.BlockSpec(memory_space=pl.ANY)] * 2,
        out_specs=whole(),
        out_shape=jax.ShapeDtypeStruct((teacher.shape[0], width), teacher.dtype),
        scratch_shapes=[
            pltpu.VMEM(teacher.shape, teacher.dtype),
            pltpu.VMEM(student.shape, student.dtype),
            pltpu.SemaphoreType.DMA((2,)),
        ],
        compiler_params=pltpu.CompilerParams(vmem_limit_bytes=mega),
        cost_estimate=cost(0, 4 * teacher.shape[0] * width),
    )(teacher, student)


def gathered(order, blocks, first, rows):
    step = 512
    for at in range(0, rows.shape[1], step):
        end = min(at + step, rows.shape[1])
        block = jnp.concatenate([x[:, first + at : first + end] for x in blocks], axis=0)
        rows[:, at:end] = jnp.dot(
            order[...], block, preferred_element_type=jnp.float32
        ).astype(jnp.bfloat16)


def logits(rows, weight, first, own, other):
    step = 512
    for at in range(0, own.shape[1], step):
        raw = jnp.dot(
            rows[...], weight[:, first + at : first + at + step], preferred_element_type=jnp.float32
        )
        own[:, at : at + step], other[:, at : at + step] = raw[:half], raw[half:]


def placed(places, which, block):
    return pl.ds(pl.multiple_of(places[which, block], 8), 8)


def teacher_early_kernel(x0, weight, out):
    step = 512
    for at in range(0, vocab_local, step):
        cols = slice(at, at + step)
        out[:, cols] = jnp.dot(
            x0[:, :teacher_width], weight[:, cols], preferred_element_type=jnp.float32
        )


def teacher_kernel(places, early, x1, x2, x3, weight, own, other, rows, raw):
    for i, x in enumerate((x1, x2, x3)):
        rows[128 * i : 128 * (i + 1)] = x[:, :teacher_width]
    step = raw.shape[2]
    for i, at in enumerate(range(0, vocab_local, step)):
        cols, held = slice(at, at + step), raw.at[i % 2]
        for block in range(16):
            held[placed(places, 0, block)] = early[8 * block : 8 * (block + 1), cols]
        term = jnp.dot(rows[...], weight[:, cols], preferred_element_type=jnp.float32)
        for block in range(48):
            held[placed(places, 0, 16 + block)] = term[8 * block : 8 * (block + 1)]
        own[:, cols], other[:, cols] = held[:half], held[half:]


def student_kernel(main_order, apart_order, *refs):
    main, separate, (weight, own, other, rows) = refs[:4], refs[4:8], refs[8:]
    gathered(apart_order, separate, 0, rows.at[:, :apart])
    gathered(main_order, main, teacher_width, rows.at[:, apart:])
    logits(rows, weight, 0, own, other)


def student_rest_kernel(rows, weight, own, other):
    logits(rows, weight, vocab_local - own.shape[1], own, other)


def own_place(token, at, axes_of, core):
    block, row = token // 8, token % 8
    for stage, axes in enumerate(axes_of):
        digit = (block >> (2 * stage)) & 3
        offset = digit ^ (digit >> 1)
        for axis in at:
            taken = (axes[0] == axis) * (1 - core) + (axes[1] == axis) * core
            at[axis] = at[axis] - taken * offset
    x, y, z = (at[axis] & 3 for axis in "xyz")
    owner = z * 16 + (x & 1) * 8 + y * 2 + (x >> 1)
    return ((owner - 32 * core) & 63) * 8 + row


def reduce_place(row, at, core):
    block = row // 8
    digit, member = block >> 4, block & 15
    offset = digit ^ (digit >> 1)
    z = (1 - core) * ((at["z"] - offset) & 3) + core * (member >> 2)
    y = (1 - core) * ((member >> 1) & 3) + core * ((at["y"] - offset) & 3)
    x_lo = (1 - core) * (member >> 3) + core * ((member >> 1) & 1)
    owner = z * 16 + x_lo * 8 + y * 2 + (member & 1)
    return ((owner - 32 * core) & 63) * 8 + row % 8


def setup_kernel(_, main_order, apart_order, places, first_core):
    core = lax.axis_index("mp")
    batch, vocab = lax.axis_index("batch"), lax.axis_index("vocab")
    at = {"x": (vocab % 2) * 2 + batch % 2, "y": vocab // 2, "z": batch // 2}
    token = lax.broadcasted_iota(jnp.int32, (1, tokens), 1)
    rows = lax.broadcasted_iota(jnp.int32, (tokens, tokens), 0)
    for order, axes_of in ((main_order, main_axes), (apart_order, apart_axes)):
        goal = own_place(token, dict(at), axes_of, core)
        order[...] = jnp.where(rows == goal, 1.0, 0.0).astype(jnp.bfloat16)
    block = lax.broadcasted_iota(jnp.int32, (1, 128), 1) % 64 * 8
    places[0:1] = own_place(block, dict(at), main_axes, core)
    places[1:2] = reduce_place(block, at, core)
    first_core[...] = jnp.full(first_core.shape, 1.0, jnp.float32) * (core == 0).astype(jnp.float32)


def setup(weight):
    order = jax.ShapeDtypeStruct((tokens, tokens), jnp.bfloat16)
    small = jax.ShapeDtypeStruct((2, 128), jnp.float32)
    return pl.pallas_call(
        setup_kernel,
        in_specs=[pl.BlockSpec(memory_space=pl.ANY)],
        out_specs=[whole()] * 4,
        out_shape=[order] * 2 + [jax.ShapeDtypeStruct((2, 128), jnp.int32), small],
        compiler_params=pltpu.CompilerParams(vmem_limit_bytes=4 * mega),
        cost_estimate=cost(0, 2 * mega),
    )(weight)


def cost(macs, moved, transcendentals=0):
    return pl.CostEstimate(flops=2 * macs, bytes_accessed=moved, transcendentals=transcendentals)


def whole():
    return pl.BlockSpec(memory_space=pltpu.VMEM)


def raw_shapes(cols):
    return [jax.ShapeDtypeStruct((half, cols), jnp.float32)] * 2


def scalars():
    return pl.BlockSpec(memory_space=pltpu.SMEM)


def teacher_early(x0, weight):
    return pl.pallas_call(
        teacher_early_kernel,
        in_specs=[whole()] * 2,
        out_specs=whole(),
        out_shape=jax.ShapeDtypeStruct((128, vocab_local), jnp.float32),
        compiler_params=pltpu.CompilerParams(vmem_limit_bytes=16 * mega),
        cost_estimate=cost(128 * weight.size, 2 * weight.size),
    )(x0, weight)


def teacher_logits(places, early, blocks, weight):
    return pl.pallas_call(
        teacher_kernel,
        in_specs=[scalars()] + [whole()] * 5,
        out_specs=[whole()] * 2,
        out_shape=raw_shapes(vocab_local),
        scratch_shapes=[
            pltpu.VMEM((384, teacher_width), jnp.bfloat16),
            pltpu.VMEM((2, tokens, 512), jnp.float32),
        ],
        compiler_params=pltpu.CompilerParams(vmem_limit_bytes=26 * mega),
        cost_estimate=cost(384 * weight.size, 2 * weight.size),
    )(places, early, *blocks, weight)


def student_logits(main_order, apart_order, main, separate, weight, cols):
    return pl.pallas_call(
        student_kernel,
        in_specs=[whole()] * 11,
        out_specs=[whole()] * 3,
        out_shape=raw_shapes(cols) + [jax.ShapeDtypeStruct((tokens, student_width), jnp.bfloat16)],
        compiler_params=pltpu.CompilerParams(vmem_limit_bytes=20 * mega),
        cost_estimate=cost(tokens * student_width * cols, 2 * weight.size),
    )(main_order, apart_order, *main, *separate, weight)


def student_rest(rows, weight, cols):
    return pl.pallas_call(
        student_rest_kernel,
        in_specs=[whole()] * 2,
        out_specs=[whole()] * 2,
        out_shape=raw_shapes(cols),
        compiler_params=pltpu.CompilerParams(vmem_limit_bytes=16 * mega),
        cost_estimate=cost(tokens * student_width * cols, 2 * weight.size),
    )(rows, weight)


def lanes(values):
    total = values[:, :128]
    for at in range(128, values.shape[1], 128):
        total += values[:, at : at + 128]
    return total


def capped_exp(own, other):
    ratio = jnp.tanh((own[...] + other[...]) * (1.0 / softcap_limit))
    return ratio, jnp.exp(softcap_limit * ratio - softcap_limit)


def teacher_statistics_kernel(own, other, tanh, exp, total):
    @pl.when(pl.program_id(0) == 0)
    def _():
        total[...] = jnp.zeros_like(total)

    tanh[...], exp[...] = capped_exp(own, other)
    total[...] += lanes(exp[...])


def teacher_statistics(own, other, tile=256):
    block = pl.BlockSpec((half, tile), lambda j: (0, j))
    return pl.pallas_call(
        teacher_statistics_kernel,
        grid=(vocab_local // tile,),
        in_specs=[block] * 2,
        out_specs=[block] * 2 + [whole()],
        out_shape=raw_shapes(vocab_local) + [jax.ShapeDtypeStruct((half, 128), jnp.float32)],
        compiler_params=pltpu.CompilerParams(vmem_limit_bytes=7 * mega),
        cost_estimate=cost(4 * half * vocab_local, 16 * half * vocab_local, 2 * half * vocab_local),
    )(own, other)


def student_statistics_kernel(last, *refs):
    before, teacher_total = refs[:2] if last else (None, None)
    tanh, exp, own, other, student_part, teacher_part, out, sums = refs[2 if last else 0 :]

    @pl.when(pl.program_id(0) == 0)
    def _():
        sums[...] = before[...] if last else jnp.zeros_like(sums)

    student_tanh, student_exp = capped_exp(own, other)
    slope = 1.0 - student_tanh * student_tanh
    student_part[...] = student_exp * slope
    teacher_part[...] = exp[...] * slope
    sums[0] += lanes(student_exp)
    sums[1] += lanes(exp[...] * (softcap_limit * (tanh[...] - student_tanh)))

    @pl.when(pl.program_id(0) == pl.num_programs(0) - 1)
    def _():
        if last:
            rows = [
                jnp.sum(total[at : at + 128].T, axis=0, keepdims=True)
                for total in (teacher_total, sums.at[0], sums.at[1])
                for at in (0, 128)
            ]
            out[...] = jnp.concatenate(rows + [jnp.zeros((2, 128), jnp.float32)], axis=0)
        else:
            out[...] = sums[...]


def student_statistics(teacher, student, first, before=None, tile=256):
    cols = student[0].shape[1]
    last = before is not None
    from_teacher = pl.BlockSpec((half, tile), lambda j: (0, first // tile + j))
    part = pl.BlockSpec((half, tile), lambda j: (0, j))
    sums = (2, half, 128)
    tanh, exp, teacher_total = teacher
    return pl.pallas_call(
        functools.partial(student_statistics_kernel, last),
        grid=(cols // tile,),
        in_specs=[whole()] * (2 * last) + [from_teacher] * 2 + [part] * 2,
        out_specs=[part, part, whole()],
        out_shape=raw_shapes(cols) + [jax.ShapeDtypeStruct((8, 128) if last else sums, jnp.float32)],
        scratch_shapes=[pltpu.VMEM(sums, jnp.float32)],
        compiler_params=pltpu.CompilerParams(vmem_limit_bytes=7 * mega),
        cost_estimate=cost(8 * half * cols, 24 * half * cols, 2 * half * cols),
    )(*([before, teacher_total] if last else []), tanh, exp, *student)


def gap_kernel(total, token_weight, student0, teacher0, student1, teacher1, gap, divergence):
    teacher_total, student_total, cross = total[0:2], total[2:4], total[4:6]
    divergence[...] = cross / teacher_total - jnp.log(teacher_total) + jnp.log(student_total)
    mine = token_weight[pl.ds(lax.axis_index("mp") * 2, 2), :]
    rows = [mine / student_total, mine / teacher_total, total[0:4]]
    scales = jnp.concatenate(rows, axis=0).T
    cols = student0.shape[1]
    for i in range(2):
        at = slice(128 * i, 128 * (i + 1))
        student_scale, teacher_scale = scales[:, i : i + 1], scales[:, 2 + i : 3 + i]
        for first, student, teacher in ((0, student0, teacher0), (cols, student1, teacher1)):
            gap[at, first : first + student.shape[1]] = (
                student[at] * student_scale - teacher[at] * teacher_scale
            ).astype(jnp.bfloat16)


def gap_of(total, token_weight, parts):
    return pl.pallas_call(
        gap_kernel,
        in_specs=[whole()] * 6,
        out_specs=[whole(), whole()],
        out_shape=[
            jax.ShapeDtypeStruct((half, vocab_local), jnp.bfloat16),
            jax.ShapeDtypeStruct((2, 128), jnp.float32),
        ],
        compiler_params=pltpu.CompilerParams(vmem_limit_bytes=4 * mega),
        cost_estimate=cost(2 * half * vocab_local, 10 * half * vocab_local),
    )(total, token_weight, *parts)


def hidden_term(gap, weight):
    return lax.dot_general(
        gap[...], weight, (((1,), (1,)), ((), ())), preferred_element_type=jnp.float32
    )


def column_tiles(tile=256):
    return [slice(at, at + tile) for at in range(0, student_width, tile)]


def hidden_own_kernel(gap, weight, out):
    for cols in column_tiles():
        out[:, cols] = hidden_term(gap, weight[cols])


def hidden_own(gap, weight):
    return pl.pallas_call(
        hidden_own_kernel,
        in_specs=[whole()] * 2,
        out_specs=whole(),
        out_shape=jax.ShapeDtypeStruct((half, student_width), jnp.float32),
        compiler_params=pltpu.CompilerParams(vmem_limit_bytes=14 * mega),
        cost_estimate=cost(half * weight.size, 2 * weight.size),
    )(gap, weight)


def hidden_all_kernel(places, own, gap, weight, keep, send1, send2, send3, term):
    for cols in column_tiles():
        term[:half, cols] = own[:, cols]
        term[half:, cols] = hidden_term(gap, weight[cols])
        for pair in range(32):
            both = [term[placed(places, 1, 2 * pair + i), cols] for i in range(2)]
            both = jnp.concatenate(both, axis=0)
            out = (keep, send1, send2, send3)[pair // 8]
            at = 16 * (pair % 8)
            out[at : at + 16, cols] = both.astype(out.dtype)


def hidden_all(places, own, gap, weight):
    return pl.pallas_call(
        hidden_all_kernel,
        in_specs=[scalars()] + [whole()] * 3,
        out_specs=[whole()] * 4,
        out_shape=[jax.ShapeDtypeStruct((128, student_width), jnp.float32)]
        + [jax.ShapeDtypeStruct((128, student_width), jnp.bfloat16)] * 3,
        scratch_shapes=[pltpu.VMEM((tokens, student_width), jnp.float32)],
        compiler_params=pltpu.CompilerParams(vmem_limit_bytes=22 * mega),
        cost_estimate=cost(half * weight.size, 2 * weight.size),
    )(places, own, gap, weight)


def first_sum_kernel(mine, *refs):
    received, out = refs[:3], refs[3]
    total = mine[...] + sum(r[...].astype(jnp.float32) for r in received)
    out[...] = total.astype(out.dtype)


def first_sum(mine, received):
    return pl.pallas_call(
        first_sum_kernel,
        in_specs=[whole()] * 4,
        out_specs=whole(),
        out_shape=jax.ShapeDtypeStruct(mine.shape, jnp.bfloat16),
        compiler_params=pltpu.CompilerParams(vmem_limit_bytes=6 * mega),
        cost_estimate=cost(128 * student_width * 4, 2 * mega),
    )(mine, *received)


def last_sum_kernel(received, out):
    total = received[0].astype(jnp.float32)
    for i in range(1, received.shape[0]):
        total += received[i].astype(jnp.float32)
    out[...] = total.astype(out.dtype)


def last_sum(received):
    return pl.pallas_call(
        last_sum_kernel,
        in_specs=[whole()],
        out_specs=whole(),
        out_shape=jax.ShapeDtypeStruct(received.shape[1:], received.dtype),
        compiler_params=pltpu.CompilerParams(vmem_limit_bytes=3 * mega),
        cost_estimate=cost(received.size, 2 * received.size),
    )(received)


def grad_weight_kernel(rows, own, other, out):
    over_rows = (((0,), (0,)), ((), ()))
    out[...] = (
        lax.dot_general(rows[:half], own[...], over_rows, preferred_element_type=jnp.float32)
        + lax.dot_general(rows[half:], other[...], over_rows, preferred_element_type=jnp.float32)
    ).astype(jnp.bfloat16)


def grad_weight_of(rows, own, other, tile=256):
    return pl.pallas_call(
        grad_weight_kernel,
        grid=(student_width // tile,),
        in_specs=[pl.BlockSpec((tokens, tile), lambda j: (0, j)), whole(), whole()],
        out_specs=pl.BlockSpec((tile, vocab_local), lambda j: (j, 0)),
        out_shape=jax.ShapeDtypeStruct((student_width, vocab_local), jnp.bfloat16),
        compiler_params=pltpu.CompilerParams(vmem_limit_bytes=9 * mega),
        cost_estimate=cost(tokens * student_width * vocab_local, 2 * student_width * vocab_local),
    )(rows, own, other)


def local(hidden_teacher, hidden_student, teacher_weight, student_weight, token_weight):
    main_order, apart_order, places, first_core = setup(teacher_weight)

    def shared_along(block, axes):
        return [block] + [send(block, axes, by) for by in offsets[1:]]

    def joined(blocks):
        return jnp.concatenate(blocks, axis=0)

    block = joined(shared_along(side_by_side(hidden_teacher, hidden_student), main_axes[0]))
    block, places = lax.optimization_barrier((block, places))
    separate, main = block[:, :apart], block[:, apart:]
    main, separate = shared_along(main, main_axes[1]), shared_along(separate, apart_axes[1])
    main = joined(main)
    _, *separate = lax.optimization_barrier((main, *separate))
    separate = joined(separate)
    main = shared_along(main, main_axes[2])
    separate = shared_along(separate, apart_axes[2])
    early = teacher_early(main[0], teacher_weight)
    teacher_own, teacher_other = teacher_logits(places, early, main[1:], teacher_weight)
    teacher_other, *separate = lax.optimization_barrier((teacher_other, *separate))
    teacher_other = swap(teacher_other)
    cols = 1536
    own0, other0, rows = student_logits(
        main_order, apart_order, main, separate, student_weight, cols
    )
    other0 = swap(other0)
    own1, other1 = student_rest(rows, student_weight, vocab_local - cols)
    teacher_own, other1 = lax.optimization_barrier((teacher_own, other1))
    other1 = swap(other1)
    teacher = teacher_statistics(teacher_own, teacher_other)
    student_part0, teacher_part0, sums = student_statistics(teacher, (own0, other0), 0)
    student_part1, teacher_part1, sums = student_statistics(teacher, (own1, other1), cols, sums)
    for axes in reduce_axes:
        sums = sum(shared_along(sums, axes))
    gap, divergence = gap_of(
        sums, token_weight.reshape(4, 128), (student_part0, teacher_part0, student_part1, teacher_part1)
    )
    gap_other, divergence_other = lax.optimization_barrier((swap(gap), swap(divergence)))

    def sent_back(sends, axes):
        far = send(sends[2], axes, -offsets[3])
        return [send(b, axes, -by) for b, by in zip(sends[:2], offsets[1:3])] + [far]

    hidden = hidden_own(gap, student_weight)
    gap_other, hidden = lax.optimization_barrier((gap_other, hidden))
    keep, *sends = hidden_all(places, hidden, gap_other, student_weight)
    received = sent_back(sends, reduce_axes[0])
    grad_weight = grad_weight_of(rows, gap, gap_other)
    keep, grad_weight = lax.optimization_barrier((keep, grad_weight))
    total = first_sum(keep, received).reshape(16, 8, student_width)
    total = lax.all_to_all(total, everyone, 0, 0, axis_index_groups=planes())
    grad_hidden = last_sum(total)

    first_core = first_core > 0.5
    divergence = jnp.concatenate(
        [
            jnp.where(first_core, divergence, divergence_other),
            jnp.where(first_core, divergence_other, divergence),
        ]
    ).reshape(tokens)
    return (divergence, grad_hidden, grad_weight)


def solution(mesh):
    placed = (
        P(("batch", "vocab"), "mp"),
        P(("batch", "vocab"), "mp"),
        P("mp", ("batch", "vocab")),
        P("mp", ("batch", "vocab")),
        P(),
    )
    return jax.shard_map(
        local,
        mesh=mesh,
        in_specs=placed,
        out_specs=(P(), P(("batch", "vocab"), "mp"), P("mp", ("batch", "vocab"))),
        check_vma=False,
    )
```

```python
import functools

import jax
import jax.numpy as jnp
import numpy as np
from jax import lax
from jax.experimental import pallas as pl
from jax.experimental.pallas import tpu as pltpu
from jax.sharding import PartitionSpec as P

softcap_limit = 30.0
tokens, teacher_width, student_width, vocab_local = 512, 2304, 1792, 2048
width = teacher_width + student_width
half = tokens // 2
apart = 1536
everyone = ("mp", "batch", "vocab")
mega = 1024 * 1024

offsets = (0, 1, 3, 2)
main_axes = (("y", "x"), ("z", "z"), ("x", "y"))
apart_axes = (("y", "x"), ("x", "y"), ("z", "z"))
reduce_axes = (("x", "y"), ("z", "x"), ("y", "z"))


def place(index):
    core, z, x_lo, y, x_hi = np.unravel_index(index, (2, 4, 2, 4, 2))
    return {"core": int(core), "x": int(2 * x_hi + x_lo), "y": int(y), "z": int(z)}


def index_of(at):
    return int(
        np.ravel_multi_index(
            (at["core"], at["z"], at["x"] % 2, at["y"], at["x"] // 2), (2, 4, 2, 4, 2)
        )
    )


def moved(at, axis, by):
    return {**at, axis: (at[axis] + by) % 4}


def ring(axes, by):
    pairs = []
    for source in range(128):
        at = place(source)
        pairs.append((source, index_of(moved(at, axes[at["core"]], by))))
    return pairs


def planes():
    groups = {}
    for index in range(128):
        at = place(index)
        groups.setdefault((at["core"], at[reduce_axes[0][at["core"]]]), []).append(index)
    return list(groups.values())


def send(block, axes, by):
    return lax.ppermute(block, everyone, ring(axes, by))


def swap(block):
    return lax.ppermute(block, "mp", [(0, 1), (1, 0)])


def side_by_side_kernel(teacher, student, out, held_teacher, held_student, arrived):
    copies = [
        pltpu.make_async_copy(teacher, held_teacher, arrived.at[0]),
        pltpu.make_async_copy(student, held_student, arrived.at[1]),
    ]
    for copy in copies:
        copy.start()
    for copy in copies:
        copy.wait()
    out[:, :apart] = held_student[:, :apart]
    out[:, apart : apart + teacher_width] = held_teacher[...]
    out[:, apart + teacher_width :] = held_student[:, apart:]


def side_by_side(teacher, student):
    return pl.pallas_call(
        side_by_side_kernel,
        in_specs=[pl.BlockSpec(memory_space=pl.ANY)] * 2,
        out_specs=whole(),
        out_shape=jax.ShapeDtypeStruct((teacher.shape[0], width), teacher.dtype),
        scratch_shapes=[
            pltpu.VMEM(teacher.shape, teacher.dtype),
            pltpu.VMEM(student.shape, student.dtype),
            pltpu.SemaphoreType.DMA((2,)),
        ],
        compiler_params=pltpu.CompilerParams(vmem_limit_bytes=mega),
        cost_estimate=cost(0, 4 * teacher.shape[0] * width),
    )(teacher, student)


def gathered(order, blocks, first, rows):
    step = 512
    for at in range(0, rows.shape[1], step):
        end = min(at + step, rows.shape[1])
        block = jnp.concatenate([x[:, first + at : first + end] for x in blocks], axis=0)
        rows[:, at:end] = jnp.dot(
            order[...], block, preferred_element_type=jnp.float32
        ).astype(jnp.bfloat16)


def logits(rows, weight, first, own, other):
    step = 512
    for at in range(0, own.shape[1], step):
        raw = jnp.dot(
            rows[...], weight[:, first + at : first + at + step], preferred_element_type=jnp.float32
        )
        own[:, at : at + step], other[:, at : at + step] = raw[:half], raw[half:]


def placed(places, which, block):
    return pl.ds(pl.multiple_of(places[which, block], 8), 8)


def teacher_early_kernel(x0, weight, out):
    step = 512
    for at in range(0, vocab_local, step):
        cols = slice(at, at + step)
        out[:, cols] = jnp.dot(
            x0[:, :teacher_width], weight[:, cols], preferred_element_type=jnp.float32
        )


def teacher_kernel(places, early, x1, x2, x3, weight, own, other, rows, raw):
    for i, x in enumerate((x1, x2, x3)):
        rows[128 * i : 128 * (i + 1)] = x[:, :teacher_width]
    step = raw.shape[2]
    for i, at in enumerate(range(0, vocab_local, step)):
        cols, held = slice(at, at + step), raw.at[i % 2]
        for block in range(16):
            held[placed(places, 0, block)] = early[8 * block : 8 * (block + 1), cols]
        term = jnp.dot(rows[...], weight[:, cols], preferred_element_type=jnp.float32)
        for block in range(48):
            held[placed(places, 0, 16 + block)] = term[8 * block : 8 * (block + 1)]
        own[:, cols], other[:, cols] = held[:half], held[half:]


def student_kernel(main_order, apart_order, *refs):
    main, separate, (weight, own, other, rows) = refs[:4], refs[4:8], refs[8:]
    gathered(apart_order, separate, 0, rows.at[:, :apart])
    gathered(main_order, main, teacher_width, rows.at[:, apart:])
    logits(rows, weight, 0, own, other)


def student_rest_kernel(rows, weight, own, other):
    logits(rows, weight, vocab_local - own.shape[1], own, other)


def own_place(token, at, axes_of, core):
    block, row = token // 8, token % 8
    for stage, axes in enumerate(axes_of):
        digit = (block >> (2 * stage)) & 3
        offset = digit ^ (digit >> 1)
        for axis in at:
            taken = (axes[0] == axis) * (1 - core) + (axes[1] == axis) * core
            at[axis] = at[axis] - taken * offset
    x, y, z = (at[axis] & 3 for axis in "xyz")
    owner = z * 16 + (x & 1) * 8 + y * 2 + (x >> 1)
    return ((owner - 32 * core) & 63) * 8 + row


def reduce_place(row, at, core):
    block = row // 8
    digit, member = block >> 4, block & 15
    offset = digit ^ (digit >> 1)
    x = (at["x"] - offset) & 3
    z = member >> 2
    y = (1 - core) * (member & 3) + core * ((at["y"] - offset) & 3)
    x_lo = (1 - core) * (x & 1) + core * ((member >> 1) & 1)
    x_hi = (1 - core) * (x >> 1) + core * (member & 1)
    owner = z * 16 + x_lo * 8 + y * 2 + x_hi
    return ((owner - 32 * core) & 63) * 8 + row % 8


def setup_kernel(_, main_order, apart_order, places, first_core):
    core = lax.axis_index("mp")
    batch, vocab = lax.axis_index("batch"), lax.axis_index("vocab")
    at = {"x": (vocab % 2) * 2 + batch % 2, "y": vocab // 2, "z": batch // 2}
    token = lax.broadcasted_iota(jnp.int32, (1, tokens), 1)
    rows = lax.broadcasted_iota(jnp.int32, (tokens, tokens), 0)
    for order, axes_of in ((main_order, main_axes), (apart_order, apart_axes)):
        goal = own_place(token, dict(at), axes_of, core)
        order[...] = jnp.where(rows == goal, 1.0, 0.0).astype(jnp.bfloat16)
    block = lax.broadcasted_iota(jnp.int32, (1, 128), 1) % 64 * 8
    places[0:1] = own_place(block, dict(at), main_axes, core)
    places[1:2] = reduce_place(block, at, core)
    first_core[...] = jnp.full(first_core.shape, 1.0, jnp.float32) * (core == 0).astype(jnp.float32)


def setup(weight):
    order = jax.ShapeDtypeStruct((tokens, tokens), jnp.bfloat16)
    small = jax.ShapeDtypeStruct((2, 128), jnp.float32)
    return pl.pallas_call(
        setup_kernel,
        in_specs=[pl.BlockSpec(memory_space=pl.ANY)],
        out_specs=[whole()] * 4,
        out_shape=[order] * 2 + [jax.ShapeDtypeStruct((2, 128), jnp.int32), small],
        compiler_params=pltpu.CompilerParams(vmem_limit_bytes=4 * mega),
        cost_estimate=cost(0, 2 * mega),
    )(weight)


def cost(macs, moved, transcendentals=0):
    return pl.CostEstimate(flops=2 * macs, bytes_accessed=moved, transcendentals=transcendentals)


def whole():
    return pl.BlockSpec(memory_space=pltpu.VMEM)


def raw_shapes(cols):
    return [jax.ShapeDtypeStruct((half, cols), jnp.float32)] * 2


def scalars():
    return pl.BlockSpec(memory_space=pltpu.SMEM)


def teacher_early(x0, weight):
    return pl.pallas_call(
        teacher_early_kernel,
        in_specs=[whole()] * 2,
        out_specs=whole(),
        out_shape=jax.ShapeDtypeStruct((128, vocab_local), jnp.float32),
        compiler_params=pltpu.CompilerParams(vmem_limit_bytes=16 * mega),
        cost_estimate=cost(128 * weight.size, 2 * weight.size),
    )(x0, weight)


def teacher_logits(places, early, blocks, weight):
    return pl.pallas_call(
        teacher_kernel,
        in_specs=[scalars()] + [whole()] * 5,
        out_specs=[whole()] * 2,
        out_shape=raw_shapes(vocab_local),
        scratch_shapes=[
            pltpu.VMEM((384, teacher_width), jnp.bfloat16),
            pltpu.VMEM((2, tokens, 512), jnp.float32),
        ],
        compiler_params=pltpu.CompilerParams(vmem_limit_bytes=26 * mega),
        cost_estimate=cost(384 * weight.size, 2 * weight.size),
    )(places, early, *blocks, weight)


def student_logits(main_order, apart_order, main, separate, weight, cols):
    return pl.pallas_call(
        student_kernel,
        in_specs=[whole()] * 11,
        out_specs=[whole()] * 3,
        out_shape=raw_shapes(cols) + [jax.ShapeDtypeStruct((tokens, student_width), jnp.bfloat16)],
        compiler_params=pltpu.CompilerParams(vmem_limit_bytes=20 * mega),
        cost_estimate=cost(tokens * student_width * cols, 2 * weight.size),
    )(main_order, apart_order, *main, *separate, weight)


def student_rest(rows, weight, cols):
    return pl.pallas_call(
        student_rest_kernel,
        in_specs=[whole()] * 2,
        out_specs=[whole()] * 2,
        out_shape=raw_shapes(cols),
        compiler_params=pltpu.CompilerParams(vmem_limit_bytes=16 * mega),
        cost_estimate=cost(tokens * student_width * cols, 2 * weight.size),
    )(rows, weight)


def lanes(values):
    total = values[:, :128]
    for at in range(128, values.shape[1], 128):
        total += values[:, at : at + 128]
    return total


def capped_exp(own, other):
    ratio = jnp.tanh((own[...] + other[...]) * (1.0 / softcap_limit))
    return ratio, jnp.exp(softcap_limit * ratio - softcap_limit)


def teacher_statistics_kernel(own, other, tanh, exp, total):
    @pl.when(pl.program_id(0) == 0)
    def _():
        total[...] = jnp.zeros_like(total)

    tanh[...], exp[...] = capped_exp(own, other)
    total[...] += lanes(exp[...])


def teacher_statistics(own, other, tile=256):
    block = pl.BlockSpec((half, tile), lambda j: (0, j))
    return pl.pallas_call(
        teacher_statistics_kernel,
        grid=(vocab_local // tile,),
        in_specs=[block] * 2,
        out_specs=[block] * 2 + [whole()],
        out_shape=raw_shapes(vocab_local) + [jax.ShapeDtypeStruct((half, 128), jnp.float32)],
        compiler_params=pltpu.CompilerParams(vmem_limit_bytes=7 * mega),
        cost_estimate=cost(4 * half * vocab_local, 16 * half * vocab_local, 2 * half * vocab_local),
    )(own, other)


def student_statistics_kernel(last, *refs):
    before, teacher_total = refs[:2] if last else (None, None)
    tanh, exp, own, other, student_part, teacher_part, out, sums = refs[2 if last else 0 :]

    @pl.when(pl.program_id(0) == 0)
    def _():
        sums[...] = before[...] if last else jnp.zeros_like(sums)

    student_tanh, student_exp = capped_exp(own, other)
    slope = 1.0 - student_tanh * student_tanh
    student_part[...] = student_exp * slope
    teacher_part[...] = exp[...] * slope
    sums[0] += lanes(student_exp)
    sums[1] += lanes(exp[...] * (softcap_limit * (tanh[...] - student_tanh)))

    @pl.when(pl.program_id(0) == pl.num_programs(0) - 1)
    def _():
        if last:
            rows = [
                jnp.sum(total[at : at + 128].T, axis=0, keepdims=True)
                for total in (teacher_total, sums.at[0], sums.at[1])
                for at in (0, 128)
            ]
            out[...] = jnp.concatenate(rows + [jnp.zeros((2, 128), jnp.float32)], axis=0)
        else:
            out[...] = sums[...]


def student_statistics(teacher, student, first, before=None, tile=256):
    cols = student[0].shape[1]
    last = before is not None
    from_teacher = pl.BlockSpec((half, tile), lambda j: (0, first // tile + j))
    part = pl.BlockSpec((half, tile), lambda j: (0, j))
    sums = (2, half, 128)
    tanh, exp, teacher_total = teacher
    return pl.pallas_call(
        functools.partial(student_statistics_kernel, last),
        grid=(cols // tile,),
        in_specs=[whole()] * (2 * last) + [from_teacher] * 2 + [part] * 2,
        out_specs=[part, part, whole()],
        out_shape=raw_shapes(cols) + [jax.ShapeDtypeStruct((8, 128) if last else sums, jnp.float32)],
        scratch_shapes=[pltpu.VMEM(sums, jnp.float32)],
        compiler_params=pltpu.CompilerParams(vmem_limit_bytes=7 * mega),
        cost_estimate=cost(8 * half * cols, 24 * half * cols, 2 * half * cols),
    )(*([before, teacher_total] if last else []), tanh, exp, *student)


def gap_kernel(total, token_weight, student0, teacher0, student1, teacher1, gap, divergence):
    teacher_total, student_total, cross = total[0:2], total[2:4], total[4:6]
    divergence[...] = cross / teacher_total - jnp.log(teacher_total) + jnp.log(student_total)
    mine = token_weight[pl.ds(lax.axis_index("mp") * 2, 2), :]
    rows = [mine / student_total, mine / teacher_total, total[0:4]]
    scales = jnp.concatenate(rows, axis=0).T
    cols = student0.shape[1]
    for i in range(2):
        at = slice(128 * i, 128 * (i + 1))
        student_scale, teacher_scale = scales[:, i : i + 1], scales[:, 2 + i : 3 + i]
        for first, student, teacher in ((0, student0, teacher0), (cols, student1, teacher1)):
            gap[at, first : first + student.shape[1]] = (
                student[at] * student_scale - teacher[at] * teacher_scale
            ).astype(jnp.bfloat16)


def gap_of(total, token_weight, parts):
    return pl.pallas_call(
        gap_kernel,
        in_specs=[whole()] * 6,
        out_specs=[whole(), whole()],
        out_shape=[
            jax.ShapeDtypeStruct((half, vocab_local), jnp.bfloat16),
            jax.ShapeDtypeStruct((2, 128), jnp.float32),
        ],
        compiler_params=pltpu.CompilerParams(vmem_limit_bytes=4 * mega),
        cost_estimate=cost(2 * half * vocab_local, 10 * half * vocab_local),
    )(total, token_weight, *parts)


def hidden_term(gap, weight):
    return lax.dot_general(
        gap[...], weight, (((1,), (1,)), ((), ())), preferred_element_type=jnp.float32
    )


def column_tiles(tile=256):
    return [slice(at, at + tile) for at in range(0, student_width, tile)]


def hidden_own_kernel(gap, weight, out):
    for cols in column_tiles():
        out[:, cols] = hidden_term(gap, weight[cols])


def hidden_own(gap, weight):
    return pl.pallas_call(
        hidden_own_kernel,
        in_specs=[whole()] * 2,
        out_specs=whole(),
        out_shape=jax.ShapeDtypeStruct((half, student_width), jnp.float32),
        compiler_params=pltpu.CompilerParams(vmem_limit_bytes=14 * mega),
        cost_estimate=cost(half * weight.size, 2 * weight.size),
    )(gap, weight)


def hidden_all_kernel(places, own, gap, weight, keep, send1, send2, send3, term):
    for cols in column_tiles():
        term[:half, cols] = own[:, cols]
        term[half:, cols] = hidden_term(gap, weight[cols])
        for pair in range(32):
            both = [term[placed(places, 1, 2 * pair + i), cols] for i in range(2)]
            both = jnp.concatenate(both, axis=0)
            out = (keep, send1, send2, send3)[pair // 8]
            at = 16 * (pair % 8)
            out[at : at + 16, cols] = both.astype(out.dtype)


def hidden_all(places, own, gap, weight):
    return pl.pallas_call(
        hidden_all_kernel,
        in_specs=[scalars()] + [whole()] * 3,
        out_specs=[whole()] * 4,
        out_shape=[jax.ShapeDtypeStruct((128, student_width), jnp.float32)]
        + [jax.ShapeDtypeStruct((128, student_width), jnp.bfloat16)] * 3,
        scratch_shapes=[pltpu.VMEM((tokens, student_width), jnp.float32)],
        compiler_params=pltpu.CompilerParams(vmem_limit_bytes=22 * mega),
        cost_estimate=cost(half * weight.size, 2 * weight.size),
    )(places, own, gap, weight)


def first_sum_kernel(mine, *refs):
    received, out = refs[:3], refs[3]
    total = mine[...] + sum(r[...].astype(jnp.float32) for r in received)
    out[...] = total.astype(out.dtype)


def first_sum(mine, received):
    return pl.pallas_call(
        first_sum_kernel,
        in_specs=[whole()] * 4,
        out_specs=whole(),
        out_shape=jax.ShapeDtypeStruct(mine.shape, jnp.bfloat16),
        compiler_params=pltpu.CompilerParams(vmem_limit_bytes=6 * mega),
        cost_estimate=cost(128 * student_width * 4, 2 * mega),
    )(mine, *received)


def last_sum_kernel(received, out):
    total = received[0].astype(jnp.float32)
    for i in range(1, received.shape[0]):
        total += received[i].astype(jnp.float32)
    out[...] = total.astype(out.dtype)


def last_sum(received):
    return pl.pallas_call(
        last_sum_kernel,
        in_specs=[whole()],
        out_specs=whole(),
        out_shape=jax.ShapeDtypeStruct(received.shape[1:], received.dtype),
        compiler_params=pltpu.CompilerParams(vmem_limit_bytes=3 * mega),
        cost_estimate=cost(received.size, 2 * received.size),
    )(received)


def grad_weight_kernel(rows, own, other, out):
    over_rows = (((0,), (0,)), ((), ()))
    out[...] = (
        lax.dot_general(rows[:half], own[...], over_rows, preferred_element_type=jnp.float32)
        + lax.dot_general(rows[half:], other[...], over_rows, preferred_element_type=jnp.float32)
    ).astype(jnp.bfloat16)


def grad_weight_of(rows, own, other, tile=256):
    return pl.pallas_call(
        grad_weight_kernel,
        grid=(student_width // tile,),
        in_specs=[pl.BlockSpec((tokens, tile), lambda j: (0, j)), whole(), whole()],
        out_specs=pl.BlockSpec((tile, vocab_local), lambda j: (j, 0)),
        out_shape=jax.ShapeDtypeStruct((student_width, vocab_local), jnp.bfloat16),
        compiler_params=pltpu.CompilerParams(vmem_limit_bytes=9 * mega),
        cost_estimate=cost(tokens * student_width * vocab_local, 2 * student_width * vocab_local),
    )(rows, own, other)


def local(hidden_teacher, hidden_student, teacher_weight, student_weight, token_weight):
    main_order, apart_order, places, first_core = setup(teacher_weight)

    def shared_along(block, axes):
        return [block] + [send(block, axes, by) for by in offsets[1:]]

    def joined(blocks):
        return jnp.concatenate(blocks, axis=0)

    block = joined(shared_along(side_by_side(hidden_teacher, hidden_student), main_axes[0]))
    block, places = lax.optimization_barrier((block, places))
    separate, main = block[:, :apart], block[:, apart:]
    main, separate = shared_along(main, main_axes[1]), shared_along(separate, apart_axes[1])
    main = joined(main)
    _, *separate = lax.optimization_barrier((main, *separate))
    separate = joined(separate)
    main = shared_along(main, main_axes[2])
    separate = shared_along(separate, apart_axes[2])
    early = teacher_early(main[0], teacher_weight)
    teacher_own, teacher_other = teacher_logits(places, early, main[1:], teacher_weight)
    teacher_other, *separate = lax.optimization_barrier((teacher_other, *separate))
    teacher_other = swap(teacher_other)
    cols = 1536
    own0, other0, rows = student_logits(
        main_order, apart_order, main, separate, student_weight, cols
    )
    other0 = swap(other0)
    own1, other1 = student_rest(rows, student_weight, vocab_local - cols)
    teacher_own, other1 = lax.optimization_barrier((teacher_own, other1))
    other1 = swap(other1)
    teacher = teacher_statistics(teacher_own, teacher_other)
    student_part0, teacher_part0, sums = student_statistics(teacher, (own0, other0), 0)
    student_part1, teacher_part1, sums = student_statistics(teacher, (own1, other1), cols, sums)
    for axes in reduce_axes:
        sums = sum(shared_along(sums, axes))
    gap, divergence = gap_of(
        sums, token_weight.reshape(4, 128), (student_part0, teacher_part0, student_part1, teacher_part1)
    )
    gap_other, divergence_other = lax.optimization_barrier((swap(gap), swap(divergence)))

    def sent_back(sends, axes):
        far = send(sends[2], axes, -offsets[3])
        return [send(b, axes, -by) for b, by in zip(sends[:2], offsets[1:3])] + [far]

    hidden = hidden_own(gap, student_weight)
    gap_other, hidden = lax.optimization_barrier((gap_other, hidden))
    keep, *sends = hidden_all(places, hidden, gap_other, student_weight)
    received = sent_back(sends, reduce_axes[0])
    grad_weight = grad_weight_of(rows, gap, gap_other)
    keep, grad_weight = lax.optimization_barrier((keep, grad_weight))
    total = first_sum(keep, received).reshape(16, 8, student_width)
    total = lax.all_to_all(total, everyone, 0, 0, axis_index_groups=planes())
    grad_hidden = last_sum(total)

    first_core = first_core > 0.5
    divergence = jnp.concatenate(
        [
            jnp.where(first_core, divergence, divergence_other),
            jnp.where(first_core, divergence_other, divergence),
        ]
    ).reshape(tokens)
    return (divergence, grad_hidden, grad_weight)


def solution(mesh):
    placed = (
        P(("batch", "vocab"), "mp"),
        P(("batch", "vocab"), "mp"),
        P("mp", ("batch", "vocab")),
        P("mp", ("batch", "vocab")),
        P(),
    )
    return jax.shard_map(
        local,
        mesh=mesh,
        in_specs=placed,
        out_specs=(P(), P(("batch", "vocab"), "mp"), P("mp", ("batch", "vocab"))),
        check_vma=False,
    )
```

```python
import functools

import jax
import jax.numpy as jnp
import numpy as np
from jax import lax
from jax.experimental import pallas as pl
from jax.experimental.pallas import tpu as pltpu
from jax.sharding import PartitionSpec as P

softcap_limit = 30.0
tokens, teacher_width, student_width, vocab_local = 512, 2304, 1792, 2048
width = teacher_width + student_width
half = tokens // 2
apart = 1536
everyone = ("mp", "batch", "vocab")
mega = 1024 * 1024

offsets = (0, 1, 3, 2)
main_axes = (("y", "x"), ("z", "z"), ("x", "y"))
apart_axes = (("y", "x"), ("x", "y"), ("z", "z"))
reduce_axes = (("x", "y"), ("z", "x"), ("y", "z"))


def place(index):
    core, z, x_lo, y, x_hi = np.unravel_index(index, (2, 4, 2, 4, 2))
    return {"core": int(core), "x": int(2 * x_hi + x_lo), "y": int(y), "z": int(z)}


def index_of(at):
    return int(
        np.ravel_multi_index(
            (at["core"], at["z"], at["x"] % 2, at["y"], at["x"] // 2), (2, 4, 2, 4, 2)
        )
    )


def moved(at, axis, by):
    return {**at, axis: (at[axis] + by) % 4}


def ring(axes, by):
    pairs = []
    for source in range(128):
        at = place(source)
        pairs.append((source, index_of(moved(at, axes[at["core"]], by))))
    return pairs


def planes():
    groups = {}
    for index in range(128):
        at = place(index)
        groups.setdefault((at["core"], at[reduce_axes[0][at["core"]]]), []).append(index)
    return list(groups.values())


def send(block, axes, by):
    return lax.ppermute(block, everyone, ring(axes, by))


def swap(block):
    return lax.ppermute(block, "mp", [(0, 1), (1, 0)])


def side_by_side_kernel(teacher, student, out, held_teacher, held_student, arrived):
    copies = [
        pltpu.make_async_copy(teacher, held_teacher, arrived.at[0]),
        pltpu.make_async_copy(student, held_student, arrived.at[1]),
    ]
    for copy in copies:
        copy.start()
    for copy in copies:
        copy.wait()
    out[:, :apart] = held_student[:, :apart]
    out[:, apart : apart + teacher_width] = held_teacher[...]
    out[:, apart + teacher_width :] = held_student[:, apart:]


def side_by_side(teacher, student):
    return pl.pallas_call(
        side_by_side_kernel,
        in_specs=[pl.BlockSpec(memory_space=pl.ANY)] * 2,
        out_specs=whole(),
        out_shape=jax.ShapeDtypeStruct((teacher.shape[0], width), teacher.dtype),
        scratch_shapes=[
            pltpu.VMEM(teacher.shape, teacher.dtype),
            pltpu.VMEM(student.shape, student.dtype),
            pltpu.SemaphoreType.DMA((2,)),
        ],
        compiler_params=pltpu.CompilerParams(vmem_limit_bytes=mega),
        cost_estimate=cost(0, 4 * teacher.shape[0] * width),
    )(teacher, student)


def gathered(order, blocks, first, rows):
    step = 512
    for at in range(0, rows.shape[1], step):
        end = min(at + step, rows.shape[1])
        block = jnp.concatenate([x[:, first + at : first + end] for x in blocks], axis=0)
        rows[:, at:end] = jnp.dot(
            order[...], block, preferred_element_type=jnp.float32
        ).astype(jnp.bfloat16)


def logits(rows, weight, first, own, other):
    step = 512
    for at in range(0, own.shape[1], step):
        raw = jnp.dot(
            rows[...], weight[:, first + at : first + at + step], preferred_element_type=jnp.float32
        )
        own[:, at : at + step], other[:, at : at + step] = raw[:half], raw[half:]


def placed(places, which, block):
    return pl.ds(pl.multiple_of(places[which, block], 8), 8)


def teacher_early_kernel(x0, weight, out):
    step = 512
    for at in range(0, vocab_local, step):
        cols = slice(at, at + step)
        out[:, cols] = jnp.dot(
            x0[:, :teacher_width], weight[:, cols], preferred_element_type=jnp.float32
        )


def teacher_kernel(places, early, x1, x2, x3, weight, own, other, rows, raw):
    for i, x in enumerate((x1, x2, x3)):
        rows[128 * i : 128 * (i + 1)] = x[:, :teacher_width]
    step = raw.shape[2]
    for i, at in enumerate(range(0, vocab_local, step)):
        cols, held = slice(at, at + step), raw.at[i % 2]
        for block in range(16):
            held[placed(places, 0, block)] = early[8 * block : 8 * (block + 1), cols]
        term = jnp.dot(rows[...], weight[:, cols], preferred_element_type=jnp.float32)
        for block in range(48):
            held[placed(places, 0, 16 + block)] = term[8 * block : 8 * (block + 1)]
        own[:, cols], other[:, cols] = held[:half], held[half:]


def student_kernel(main_order, apart_order, *refs):
    main, separate, (weight, own, other, rows) = refs[:4], refs[4:8], refs[8:]
    gathered(apart_order, separate, 0, rows.at[:, :apart])
    gathered(main_order, main, teacher_width, rows.at[:, apart:])
    logits(rows, weight, 0, own, other)


def student_rest_kernel(rows, weight, own, other):
    logits(rows, weight, vocab_local - own.shape[1], own, other)


def own_place(token, at, axes_of, core):
    block, row = token // 8, token % 8
    for stage, axes in enumerate(axes_of):
        digit = (block >> (2 * stage)) & 3
        offset = digit ^ (digit >> 1)
        for axis in at:
            taken = (axes[0] == axis) * (1 - core) + (axes[1] == axis) * core
            at[axis] = at[axis] - taken * offset
    x, y, z = (at[axis] & 3 for axis in "xyz")
    owner = z * 16 + (x & 1) * 8 + y * 2 + (x >> 1)
    return ((owner - 32 * core) & 63) * 8 + row


def reduce_place(row, at, core):
    block = row // 8
    digit, member = block >> 4, block & 15
    offset = digit ^ (digit >> 1)
    x = (at["x"] - offset) & 3
    z = member >> 2
    y = (1 - core) * (member & 3) + core * ((at["y"] - offset) & 3)
    x_lo = (1 - core) * (x & 1) + core * ((member >> 1) & 1)
    x_hi = (1 - core) * (x >> 1) + core * (member & 1)
    owner = z * 16 + x_lo * 8 + y * 2 + x_hi
    return ((owner - 32 * core) & 63) * 8 + row % 8


def setup_kernel(_, main_order, apart_order, places, first_core):
    core = lax.axis_index("mp")
    batch, vocab = lax.axis_index("batch"), lax.axis_index("vocab")
    at = {"x": (vocab % 2) * 2 + batch % 2, "y": vocab // 2, "z": batch // 2}
    token = lax.broadcasted_iota(jnp.int32, (1, tokens), 1)
    rows = lax.broadcasted_iota(jnp.int32, (tokens, tokens), 0)
    for order, axes_of in ((main_order, main_axes), (apart_order, apart_axes)):
        goal = own_place(token, dict(at), axes_of, core)
        order[...] = jnp.where(rows == goal, 1.0, 0.0).astype(jnp.bfloat16)
    block = lax.broadcasted_iota(jnp.int32, (1, 128), 1) % 64 * 8
    places[0:1] = own_place(block, dict(at), main_axes, core)
    places[1:2] = reduce_place(block, at, core)
    first_core[...] = jnp.full(first_core.shape, 1.0, jnp.float32) * (core == 0).astype(jnp.float32)


def setup(weight):
    order = jax.ShapeDtypeStruct((tokens, tokens), jnp.bfloat16)
    small = jax.ShapeDtypeStruct((2, 128), jnp.float32)
    return pl.pallas_call(
        setup_kernel,
        in_specs=[pl.BlockSpec(memory_space=pl.ANY)],
        out_specs=[whole()] * 4,
        out_shape=[order] * 2 + [jax.ShapeDtypeStruct((2, 128), jnp.int32), small],
        compiler_params=pltpu.CompilerParams(vmem_limit_bytes=4 * mega),
        cost_estimate=cost(0, 2 * mega),
    )(weight)


def cost(macs, moved, transcendentals=0):
    return pl.CostEstimate(flops=2 * macs, bytes_accessed=moved, transcendentals=transcendentals)


def whole():
    return pl.BlockSpec(memory_space=pltpu.VMEM)


def raw_shapes(cols):
    return [jax.ShapeDtypeStruct((half, cols), jnp.float32)] * 2


def scalars():
    return pl.BlockSpec(memory_space=pltpu.SMEM)


def teacher_early(x0, weight):
    return pl.pallas_call(
        teacher_early_kernel,
        in_specs=[whole()] * 2,
        out_specs=whole(),
        out_shape=jax.ShapeDtypeStruct((128, vocab_local), jnp.float32),
        compiler_params=pltpu.CompilerParams(vmem_limit_bytes=16 * mega),
        cost_estimate=cost(128 * weight.size, 2 * weight.size),
    )(x0, weight)


def teacher_logits(places, early, blocks, weight):
    return pl.pallas_call(
        teacher_kernel,
        in_specs=[scalars()] + [whole()] * 5,
        out_specs=[whole()] * 2,
        out_shape=raw_shapes(vocab_local),
        scratch_shapes=[
            pltpu.VMEM((384, teacher_width), jnp.bfloat16),
            pltpu.VMEM((2, tokens, 512), jnp.float32),
        ],
        compiler_params=pltpu.CompilerParams(vmem_limit_bytes=26 * mega),
        cost_estimate=cost(384 * weight.size, 2 * weight.size),
    )(places, early, *blocks, weight)


def student_logits(main_order, apart_order, main, separate, weight, cols):
    return pl.pallas_call(
        student_kernel,
        in_specs=[whole()] * 11,
        out_specs=[whole()] * 3,
        out_shape=raw_shapes(cols) + [jax.ShapeDtypeStruct((tokens, student_width), jnp.bfloat16)],
        compiler_params=pltpu.CompilerParams(vmem_limit_bytes=20 * mega),
        cost_estimate=cost(tokens * student_width * cols, 2 * weight.size),
    )(main_order, apart_order, *main, *separate, weight)


def student_rest(rows, weight, cols):
    return pl.pallas_call(
        student_rest_kernel,
        in_specs=[whole()] * 2,
        out_specs=[whole()] * 2,
        out_shape=raw_shapes(cols),
        compiler_params=pltpu.CompilerParams(vmem_limit_bytes=16 * mega),
        cost_estimate=cost(tokens * student_width * cols, 2 * weight.size),
    )(rows, weight)


def lanes(values):
    total = values[:, :128]
    for at in range(128, values.shape[1], 128):
        total += values[:, at : at + 128]
    return total


def capped_exp(own, other):
    ratio = jnp.tanh((own[...] + other[...]) * (1.0 / softcap_limit))
    return ratio, jnp.exp(softcap_limit * ratio - softcap_limit)


def teacher_statistics_kernel(own, other, tanh, exp, total):
    @pl.when(pl.program_id(0) == 0)
    def _():
        total[...] = jnp.zeros_like(total)

    tanh[...], exp[...] = capped_exp(own, other)
    total[...] += lanes(exp[...])


def teacher_statistics(own, other, tile=256):
    block = pl.BlockSpec((half, tile), lambda j: (0, j))
    return pl.pallas_call(
        teacher_statistics_kernel,
        grid=(vocab_local // tile,),
        in_specs=[block] * 2,
        out_specs=[block] * 2 + [whole()],
        out_shape=raw_shapes(vocab_local) + [jax.ShapeDtypeStruct((half, 128), jnp.float32)],
        compiler_params=pltpu.CompilerParams(vmem_limit_bytes=7 * mega),
        cost_estimate=cost(4 * half * vocab_local, 16 * half * vocab_local, 2 * half * vocab_local),
    )(own, other)


def student_statistics_kernel(last, *refs):
    before, teacher_total = refs[:2] if last else (None, None)
    tanh, exp, own, other, student_part, teacher_part, out, sums = refs[2 if last else 0 :]

    @pl.when(pl.program_id(0) == 0)
    def _():
        sums[...] = before[...] if last else jnp.zeros_like(sums)

    student_tanh, student_exp = capped_exp(own, other)
    slope = 1.0 - student_tanh * student_tanh
    student_part[...] = student_exp * slope
    teacher_part[...] = exp[...] * slope
    sums[0] += lanes(student_exp)
    sums[1] += lanes(exp[...] * (softcap_limit * (tanh[...] - student_tanh)))

    @pl.when(pl.program_id(0) == pl.num_programs(0) - 1)
    def _():
        if last:
            rows = [
                jnp.sum(total[at : at + 128].T, axis=0, keepdims=True)
                for total in (teacher_total, sums.at[0], sums.at[1])
                for at in (0, 128)
            ]
            out[...] = jnp.concatenate(rows + [jnp.zeros((2, 128), jnp.float32)], axis=0)
        else:
            out[...] = sums[...]


def student_statistics(teacher, student, first, before=None, tile=256):
    cols = student[0].shape[1]
    last = before is not None
    from_teacher = pl.BlockSpec((half, tile), lambda j: (0, first // tile + j))
    part = pl.BlockSpec((half, tile), lambda j: (0, j))
    sums = (2, half, 128)
    tanh, exp, teacher_total = teacher
    return pl.pallas_call(
        functools.partial(student_statistics_kernel, last),
        grid=(cols // tile,),
        in_specs=[whole()] * (2 * last) + [from_teacher] * 2 + [part] * 2,
        out_specs=[part, part, whole()],
        out_shape=raw_shapes(cols) + [jax.ShapeDtypeStruct((8, 128) if last else sums, jnp.float32)],
        scratch_shapes=[pltpu.VMEM(sums, jnp.float32)],
        compiler_params=pltpu.CompilerParams(vmem_limit_bytes=7 * mega),
        cost_estimate=cost(8 * half * cols, 24 * half * cols, 2 * half * cols),
    )(*([before, teacher_total] if last else []), tanh, exp, *student)


def gap_kernel(total, token_weight, student0, teacher0, student1, teacher1, gap, divergence):
    teacher_total, student_total, cross = total[0:2], total[2:4], total[4:6]
    divergence[...] = cross / teacher_total - jnp.log(teacher_total) + jnp.log(student_total)
    mine = token_weight[pl.ds(lax.axis_index("mp") * 2, 2), :]
    rows = [mine / student_total, mine / teacher_total, total[0:4]]
    scales = jnp.concatenate(rows, axis=0).T
    cols = student0.shape[1]
    for i in range(2):
        at = slice(128 * i, 128 * (i + 1))
        student_scale, teacher_scale = scales[:, i : i + 1], scales[:, 2 + i : 3 + i]
        for first, student, teacher in ((0, student0, teacher0), (cols, student1, teacher1)):
            gap[at, first : first + student.shape[1]] = (
                student[at] * student_scale - teacher[at] * teacher_scale
            ).astype(jnp.bfloat16)


def gap_of(total, token_weight, parts):
    return pl.pallas_call(
        gap_kernel,
        in_specs=[whole()] * 6,
        out_specs=[whole(), whole()],
        out_shape=[
            jax.ShapeDtypeStruct((half, vocab_local), jnp.bfloat16),
            jax.ShapeDtypeStruct((2, 128), jnp.float32),
        ],
        compiler_params=pltpu.CompilerParams(vmem_limit_bytes=4 * mega),
        cost_estimate=cost(2 * half * vocab_local, 10 * half * vocab_local),
    )(total, token_weight, *parts)


def hidden_term(gap, weight):
    return lax.dot_general(
        gap[...], weight, (((1,), (1,)), ((), ())), preferred_element_type=jnp.float32
    )


def column_tiles(tile=256):
    return [slice(at, at + tile) for at in range(0, student_width, tile)]


def hidden_own_kernel(gap, weight, out):
    for cols in column_tiles():
        out[:, cols] = hidden_term(gap, weight[cols])


def hidden_own(gap, weight):
    return pl.pallas_call(
        hidden_own_kernel,
        in_specs=[whole()] * 2,
        out_specs=whole(),
        out_shape=jax.ShapeDtypeStruct((half, student_width), jnp.float32),
        compiler_params=pltpu.CompilerParams(vmem_limit_bytes=14 * mega),
        cost_estimate=cost(half * weight.size, 2 * weight.size),
    )(gap, weight)


def hidden_all_kernel(places, own, gap, weight, keep, send1, send2, send3, term):
    for cols in column_tiles():
        term[:half, cols] = own[:, cols]
        term[half:, cols] = hidden_term(gap, weight[cols])
        for pair in range(32):
            both = [term[placed(places, 1, 2 * pair + i), cols] for i in range(2)]
            both = jnp.concatenate(both, axis=0)
            out = (keep, send1, send2, send3)[pair // 8]
            at = 16 * (pair % 8)
            out[at : at + 16, cols] = both.astype(out.dtype)


def hidden_all(places, own, gap, weight):
    return pl.pallas_call(
        hidden_all_kernel,
        in_specs=[scalars()] + [whole()] * 3,
        out_specs=[whole()] * 4,
        out_shape=[jax.ShapeDtypeStruct((128, student_width), jnp.float32)]
        + [jax.ShapeDtypeStruct((128, student_width), jnp.bfloat16)] * 3,
        scratch_shapes=[pltpu.VMEM((tokens, student_width), jnp.float32)],
        compiler_params=pltpu.CompilerParams(vmem_limit_bytes=22 * mega),
        cost_estimate=cost(half * weight.size, 2 * weight.size),
    )(places, own, gap, weight)


def first_sum_kernel(mine, *refs):
    received, out = refs[:3], refs[3]
    total = mine[...] + sum(r[...].astype(jnp.float32) for r in received)
    out[...] = total.astype(out.dtype)


def first_sum(mine, received):
    return pl.pallas_call(
        first_sum_kernel,
        in_specs=[whole()] * 4,
        out_specs=whole(),
        out_shape=jax.ShapeDtypeStruct(mine.shape, jnp.bfloat16),
        compiler_params=pltpu.CompilerParams(vmem_limit_bytes=6 * mega),
        cost_estimate=cost(128 * student_width * 4, 2 * mega),
    )(mine, *received)


def last_sum_kernel(received, out):
    total = received[0].astype(jnp.float32)
    for i in range(1, received.shape[0]):
        total += received[i].astype(jnp.float32)
    out[...] = total.astype(out.dtype)


def last_sum(received):
    return pl.pallas_call(
        last_sum_kernel,
        in_specs=[whole()],
        out_specs=whole(),
        out_shape=jax.ShapeDtypeStruct(received.shape[1:], received.dtype),
        compiler_params=pltpu.CompilerParams(vmem_limit_bytes=3 * mega),
        cost_estimate=cost(received.size, 2 * received.size),
    )(received)


def grad_weight_kernel(rows, own, other, out):
    over_rows = (((0,), (0,)), ((), ()))
    out[...] = (
        lax.dot_general(rows[:half], own[...], over_rows, preferred_element_type=jnp.float32)
        + lax.dot_general(rows[half:], other[...], over_rows, preferred_element_type=jnp.float32)
    ).astype(jnp.bfloat16)


def grad_weight_of(rows, own, other, tile=256):
    return pl.pallas_call(
        grad_weight_kernel,
        grid=(student_width // tile,),
        in_specs=[pl.BlockSpec((tokens, tile), lambda j: (0, j)), whole(), whole()],
        out_specs=pl.BlockSpec((tile, vocab_local), lambda j: (j, 0)),
        out_shape=jax.ShapeDtypeStruct((student_width, vocab_local), jnp.bfloat16),
        compiler_params=pltpu.CompilerParams(vmem_limit_bytes=9 * mega),
        cost_estimate=cost(tokens * student_width * vocab_local, 2 * student_width * vocab_local),
    )(rows, own, other)


def local(hidden_teacher, hidden_student, teacher_weight, student_weight, token_weight):
    main_order, apart_order, places, first_core = setup(teacher_weight)

    def shared_along(block, axes):
        return [block] + [send(block, axes, by) for by in offsets[1:]]

    def joined(blocks):
        return jnp.concatenate(blocks, axis=0)

    block = joined(shared_along(side_by_side(hidden_teacher, hidden_student), main_axes[0]))
    block, places = lax.optimization_barrier((block, places))
    separate, main = block[:, :apart], block[:, apart:]
    main, separate = shared_along(main, main_axes[1]), shared_along(separate, apart_axes[1])
    main = joined(main)
    _, *separate = lax.optimization_barrier((main, *separate))
    separate = joined(separate)
    main = shared_along(main, main_axes[2])
    separate = shared_along(separate, apart_axes[2])
    early = teacher_early(main[0], teacher_weight)
    teacher_own, teacher_other = teacher_logits(places, early, main[1:], teacher_weight)
    teacher_other, *separate = lax.optimization_barrier((teacher_other, *separate))
    teacher_other = swap(teacher_other)
    cols = 1024
    own0, other0, rows = student_logits(
        main_order, apart_order, main, separate, student_weight, cols
    )
    other0 = swap(other0)
    own1, other1 = student_rest(rows, student_weight, vocab_local - cols)
    teacher_own, other1 = lax.optimization_barrier((teacher_own, other1))
    other1 = swap(other1)
    teacher = teacher_statistics(teacher_own, teacher_other)
    student_part0, teacher_part0, sums = student_statistics(teacher, (own0, other0), 0)
    student_part1, teacher_part1, sums = student_statistics(teacher, (own1, other1), cols, sums)
    for axes in reduce_axes:
        sums = sum(shared_along(sums, axes))
    gap, divergence = gap_of(
        sums, token_weight.reshape(4, 128), (student_part0, teacher_part0, student_part1, teacher_part1)
    )
    gap_other, divergence_other = lax.optimization_barrier((swap(gap), swap(divergence)))

    def sent_back(sends, axes):
        far = send(sends[2], axes, -offsets[3])
        return [send(b, axes, -by) for b, by in zip(sends[:2], offsets[1:3])] + [far]

    hidden = hidden_own(gap, student_weight)
    gap_other, hidden = lax.optimization_barrier((gap_other, hidden))
    keep, *sends = hidden_all(places, hidden, gap_other, student_weight)
    received = sent_back(sends, reduce_axes[0])
    grad_weight = grad_weight_of(rows, gap, gap_other)
    keep, grad_weight = lax.optimization_barrier((keep, grad_weight))
    total = first_sum(keep, received).reshape(16, 8, student_width)
    total = lax.all_to_all(total, everyone, 0, 0, axis_index_groups=planes())
    grad_hidden = last_sum(total)

    first_core = first_core > 0.5
    divergence = jnp.concatenate(
        [
            jnp.where(first_core, divergence, divergence_other),
            jnp.where(first_core, divergence_other, divergence),
        ]
    ).reshape(tokens)
    return (divergence, grad_hidden, grad_weight)


def solution(mesh):
    placed = (
        P(("batch", "vocab"), "mp"),
        P(("batch", "vocab"), "mp"),
        P("mp", ("batch", "vocab")),
        P("mp", ("batch", "vocab")),
        P(),
    )
    return jax.shard_map(
        local,
        mesh=mesh,
        in_specs=placed,
        out_specs=(P(), P(("batch", "vocab"), "mp"), P("mp", ("batch", "vocab"))),
        check_vma=False,
    )
```

```python
import functools

import jax
import jax.numpy as jnp
import numpy as np
from jax import lax
from jax.experimental import pallas as pl
from jax.experimental.pallas import tpu as pltpu
from jax.sharding import PartitionSpec as P

softcap_limit = 30.0
tokens, teacher_width, student_width, vocab_local = 512, 2304, 1792, 2048
width = teacher_width + student_width
half = tokens // 2
apart = 1536
everyone = ("mp", "batch", "vocab")
mega = 1024 * 1024

offsets = (0, 1, 3, 2)
main_axes = (("y", "x"), ("z", "z"), ("x", "y"))
apart_axes = (("y", "x"), ("x", "y"), ("z", "z"))
reduce_axes = (("x", "y"), ("z", "x"), ("y", "z"))


def place(index):
    core, z, x_lo, y, x_hi = np.unravel_index(index, (2, 4, 2, 4, 2))
    return {"core": int(core), "x": int(2 * x_hi + x_lo), "y": int(y), "z": int(z)}


def index_of(at):
    return int(
        np.ravel_multi_index(
            (at["core"], at["z"], at["x"] % 2, at["y"], at["x"] // 2), (2, 4, 2, 4, 2)
        )
    )


def moved(at, axis, by):
    return {**at, axis: (at[axis] + by) % 4}


def ring(axes, by):
    pairs = []
    for source in range(128):
        at = place(source)
        pairs.append((source, index_of(moved(at, axes[at["core"]], by))))
    return pairs


def planes():
    groups = {}
    for index in range(128):
        at = place(index)
        groups.setdefault((at["core"], at[reduce_axes[0][at["core"]]]), []).append(index)
    return list(groups.values())


def send(block, axes, by):
    return lax.ppermute(block, everyone, ring(axes, by))


def swap(block):
    return lax.ppermute(block, "mp", [(0, 1), (1, 0)])


def side_by_side_kernel(teacher, student, out, held_teacher, held_student, arrived):
    copies = [
        pltpu.make_async_copy(teacher, held_teacher, arrived.at[0]),
        pltpu.make_async_copy(student, held_student, arrived.at[1]),
    ]
    for copy in copies:
        copy.start()
    for copy in copies:
        copy.wait()
    out[:, :apart] = held_student[:, :apart]
    out[:, apart : apart + teacher_width] = held_teacher[...]
    out[:, apart + teacher_width :] = held_student[:, apart:]


def side_by_side(teacher, student):
    return pl.pallas_call(
        side_by_side_kernel,
        in_specs=[pl.BlockSpec(memory_space=pl.ANY)] * 2,
        out_specs=whole(),
        out_shape=jax.ShapeDtypeStruct((teacher.shape[0], width), teacher.dtype),
        scratch_shapes=[
            pltpu.VMEM(teacher.shape, teacher.dtype),
            pltpu.VMEM(student.shape, student.dtype),
            pltpu.SemaphoreType.DMA((2,)),
        ],
        compiler_params=pltpu.CompilerParams(vmem_limit_bytes=mega),
        cost_estimate=cost(0, 4 * teacher.shape[0] * width),
    )(teacher, student)


def gathered(order, blocks, first, rows):
    step = 512
    for at in range(0, rows.shape[1], step):
        end = min(at + step, rows.shape[1])
        block = jnp.concatenate([x[:, first + at : first + end] for x in blocks], axis=0)
        rows[:, at:end] = jnp.dot(
            order[...], block, preferred_element_type=jnp.float32
        ).astype(jnp.bfloat16)


def logits(rows, weight, first, own, other):
    step = 512
    for at in range(0, own.shape[1], step):
        raw = jnp.dot(
            rows[...], weight[:, first + at : first + at + step], preferred_element_type=jnp.float32
        )
        own[:, at : at + step], other[:, at : at + step] = raw[:half], raw[half:]


def placed(places, which, block):
    return pl.ds(pl.multiple_of(places[which, block], 8), 8)


def teacher_early_kernel(x0, weight, out):
    step = 512
    for at in range(0, vocab_local, step):
        cols = slice(at, at + step)
        out[:, cols] = jnp.dot(
            x0[:, :teacher_width], weight[:, cols], preferred_element_type=jnp.float32
        )


def teacher_kernel(places, early, x1, x2, x3, weight, own, other, rows, raw):
    for i, x in enumerate((x1, x2, x3)):
        rows[128 * i : 128 * (i + 1)] = x[:, :teacher_width]
    step = raw.shape[2]
    for i, at in enumerate(range(0, vocab_local, step)):
        cols, held = slice(at, at + step), raw.at[i % 2]
        for block in range(16):
            held[placed(places, 0, block)] = early[8 * block : 8 * (block + 1), cols]
        term = jnp.dot(rows[...], weight[:, cols], preferred_element_type=jnp.float32)
        for block in range(48):
            held[placed(places, 0, 16 + block)] = term[8 * block : 8 * (block + 1)]
        own[:, cols], other[:, cols] = held[:half], held[half:]


def student_kernel(main_order, apart_order, *refs):
    main, separate, (weight, own, other, rows) = refs[:4], refs[4:8], refs[8:]
    gathered(apart_order, separate, 0, rows.at[:, :apart])
    gathered(main_order, main, teacher_width, rows.at[:, apart:])
    logits(rows, weight, 0, own, other)


def student_rest_kernel(rows, weight, own, other):
    logits(rows, weight, vocab_local - own.shape[1], own, other)


def own_place(token, at, axes_of, core):
    block, row = token // 8, token % 8
    for stage, axes in enumerate(axes_of):
        digit = (block >> (2 * stage)) & 3
        offset = digit ^ (digit >> 1)
        for axis in at:
            taken = (axes[0] == axis) * (1 - core) + (axes[1] == axis) * core
            at[axis] = at[axis] - taken * offset
    x, y, z = (at[axis] & 3 for axis in "xyz")
    owner = z * 16 + (x & 1) * 8 + y * 2 + (x >> 1)
    return ((owner - 32 * core) & 63) * 8 + row


def reduce_place(row, at, core):
    block = row // 8
    digit, member = block >> 4, block & 15
    offset = digit ^ (digit >> 1)
    x = (at["x"] - offset) & 3
    z = member >> 2
    y = (1 - core) * (member & 3) + core * ((at["y"] - offset) & 3)
    x_lo = (1 - core) * (x & 1) + core * ((member >> 1) & 1)
    x_hi = (1 - core) * (x >> 1) + core * (member & 1)
    owner = z * 16 + x_lo * 8 + y * 2 + x_hi
    return ((owner - 32 * core) & 63) * 8 + row % 8


def setup_kernel(_, main_order, apart_order, places, first_core):
    core = lax.axis_index("mp")
    batch, vocab = lax.axis_index("batch"), lax.axis_index("vocab")
    at = {"x": (vocab % 2) * 2 + batch % 2, "y": vocab // 2, "z": batch // 2}
    token = lax.broadcasted_iota(jnp.int32, (1, tokens), 1)
    rows = lax.broadcasted_iota(jnp.int32, (tokens, tokens), 0)
    for order, axes_of in ((main_order, main_axes), (apart_order, apart_axes)):
        goal = own_place(token, dict(at), axes_of, core)
        order[...] = jnp.where(rows == goal, 1.0, 0.0).astype(jnp.bfloat16)
    block = lax.broadcasted_iota(jnp.int32, (1, 128), 1) % 64 * 8
    places[0:1] = own_place(block, dict(at), main_axes, core)
    places[1:2] = reduce_place(block, at, core)
    first_core[...] = jnp.full(first_core.shape, 1.0, jnp.float32) * (core == 0).astype(jnp.float32)


def setup(weight):
    order = jax.ShapeDtypeStruct((tokens, tokens), jnp.bfloat16)
    small = jax.ShapeDtypeStruct((2, 128), jnp.float32)
    return pl.pallas_call(
        setup_kernel,
        in_specs=[pl.BlockSpec(memory_space=pl.ANY)],
        out_specs=[whole()] * 4,
        out_shape=[order] * 2 + [jax.ShapeDtypeStruct((2, 128), jnp.int32), small],
        compiler_params=pltpu.CompilerParams(vmem_limit_bytes=4 * mega),
        cost_estimate=cost(0, 2 * mega),
    )(weight)


def cost(macs, moved, transcendentals=0):
    return pl.CostEstimate(flops=2 * macs, bytes_accessed=moved, transcendentals=transcendentals)


def whole():
    return pl.BlockSpec(memory_space=pltpu.VMEM)


def raw_shapes(cols):
    return [jax.ShapeDtypeStruct((half, cols), jnp.float32)] * 2


def scalars():
    return pl.BlockSpec(memory_space=pltpu.SMEM)


def teacher_early(x0, weight):
    return pl.pallas_call(
        teacher_early_kernel,
        in_specs=[whole()] * 2,
        out_specs=whole(),
        out_shape=jax.ShapeDtypeStruct((128, vocab_local), jnp.float32),
        compiler_params=pltpu.CompilerParams(vmem_limit_bytes=16 * mega),
        cost_estimate=cost(128 * weight.size, 2 * weight.size),
    )(x0, weight)


def teacher_logits(places, early, blocks, weight):
    return pl.pallas_call(
        teacher_kernel,
        in_specs=[scalars()] + [whole()] * 5,
        out_specs=[whole()] * 2,
        out_shape=raw_shapes(vocab_local),
        scratch_shapes=[
            pltpu.VMEM((384, teacher_width), jnp.bfloat16),
            pltpu.VMEM((2, tokens, 512), jnp.float32),
        ],
        compiler_params=pltpu.CompilerParams(vmem_limit_bytes=26 * mega),
        cost_estimate=cost(384 * weight.size, 2 * weight.size),
    )(places, early, *blocks, weight)


def student_logits(main_order, apart_order, main, separate, weight, cols):
    return pl.pallas_call(
        student_kernel,
        in_specs=[whole()] * 11,
        out_specs=[whole()] * 3,
        out_shape=raw_shapes(cols) + [jax.ShapeDtypeStruct((tokens, student_width), jnp.bfloat16)],
        compiler_params=pltpu.CompilerParams(vmem_limit_bytes=20 * mega),
        cost_estimate=cost(tokens * student_width * cols, 2 * weight.size),
    )(main_order, apart_order, *main, *separate, weight)


def student_rest(rows, weight, cols):
    return pl.pallas_call(
        student_rest_kernel,
        in_specs=[whole()] * 2,
        out_specs=[whole()] * 2,
        out_shape=raw_shapes(cols),
        compiler_params=pltpu.CompilerParams(vmem_limit_bytes=16 * mega),
        cost_estimate=cost(tokens * student_width * cols, 2 * weight.size),
    )(rows, weight)


def lanes(values):
    total = values[:, :128]
    for at in range(128, values.shape[1], 128):
        total += values[:, at : at + 128]
    return total


def capped_exp(own, other):
    ratio = jnp.tanh((own[...] + other[...]) * (1.0 / softcap_limit))
    return ratio, jnp.exp(softcap_limit * ratio - softcap_limit)


def teacher_statistics_kernel(own, other, tanh, exp, total):
    @pl.when(pl.program_id(0) == 0)
    def _():
        total[...] = jnp.zeros_like(total)

    tanh[...], exp[...] = capped_exp(own, other)
    total[...] += lanes(exp[...])


def teacher_statistics(own, other, tile=256):
    block = pl.BlockSpec((half, tile), lambda j: (0, j))
    return pl.pallas_call(
        teacher_statistics_kernel,
        grid=(vocab_local // tile,),
        in_specs=[block] * 2,
        out_specs=[block] * 2 + [whole()],
        out_shape=raw_shapes(vocab_local) + [jax.ShapeDtypeStruct((half, 128), jnp.float32)],
        compiler_params=pltpu.CompilerParams(vmem_limit_bytes=7 * mega),
        cost_estimate=cost(4 * half * vocab_local, 16 * half * vocab_local, 2 * half * vocab_local),
    )(own, other)


def student_statistics_kernel(last, *refs):
    before, teacher_total = refs[:2] if last else (None, None)
    tanh, exp, own, other, student_part, teacher_part, out, sums = refs[2 if last else 0 :]

    @pl.when(pl.program_id(0) == 0)
    def _():
        sums[...] = before[...] if last else jnp.zeros_like(sums)

    student_tanh, student_exp = capped_exp(own, other)
    slope = 1.0 - student_tanh * student_tanh
    student_part[...] = student_exp * slope
    teacher_part[...] = exp[...] * slope
    sums[0] += lanes(student_exp)
    sums[1] += lanes(exp[...] * (softcap_limit * (tanh[...] - student_tanh)))

    @pl.when(pl.program_id(0) == pl.num_programs(0) - 1)
    def _():
        if last:
            rows = [
                jnp.sum(total[at : at + 128].T, axis=0, keepdims=True)
                for total in (teacher_total, sums.at[0], sums.at[1])
                for at in (0, 128)
            ]
            out[...] = jnp.concatenate(rows + [jnp.zeros((2, 128), jnp.float32)], axis=0)
        else:
            out[...] = sums[...]


def student_statistics(teacher, student, first, before=None, tile=256):
    cols = student[0].shape[1]
    last = before is not None
    from_teacher = pl.BlockSpec((half, tile), lambda j: (0, first // tile + j))
    part = pl.BlockSpec((half, tile), lambda j: (0, j))
    sums = (2, half, 128)
    tanh, exp, teacher_total = teacher
    return pl.pallas_call(
        functools.partial(student_statistics_kernel, last),
        grid=(cols // tile,),
        in_specs=[whole()] * (2 * last) + [from_teacher] * 2 + [part] * 2,
        out_specs=[part, part, whole()],
        out_shape=raw_shapes(cols) + [jax.ShapeDtypeStruct((8, 128) if last else sums, jnp.float32)],
        scratch_shapes=[pltpu.VMEM(sums, jnp.float32)],
        compiler_params=pltpu.CompilerParams(vmem_limit_bytes=7 * mega),
        cost_estimate=cost(8 * half * cols, 24 * half * cols, 2 * half * cols),
    )(*([before, teacher_total] if last else []), tanh, exp, *student)


def gap_kernel(total, token_weight, student0, teacher0, student1, teacher1, gap, divergence):
    teacher_total, student_total, cross = total[0:2], total[2:4], total[4:6]
    divergence[...] = cross / teacher_total - jnp.log(teacher_total) + jnp.log(student_total)
    mine = token_weight[pl.ds(lax.axis_index("mp") * 2, 2), :]
    rows = [mine / student_total, mine / teacher_total, total[0:4]]
    scales = jnp.concatenate(rows, axis=0).T
    cols = student0.shape[1]
    for i in range(2):
        at = slice(128 * i, 128 * (i + 1))
        student_scale, teacher_scale = scales[:, i : i + 1], scales[:, 2 + i : 3 + i]
        for first, student, teacher in ((0, student0, teacher0), (cols, student1, teacher1)):
            gap[at, first : first + student.shape[1]] = (
                student[at] * student_scale - teacher[at] * teacher_scale
            ).astype(jnp.bfloat16)


def gap_of(total, token_weight, parts):
    return pl.pallas_call(
        gap_kernel,
        in_specs=[whole()] * 6,
        out_specs=[whole(), whole()],
        out_shape=[
            jax.ShapeDtypeStruct((half, vocab_local), jnp.bfloat16),
            jax.ShapeDtypeStruct((2, 128), jnp.float32),
        ],
        compiler_params=pltpu.CompilerParams(vmem_limit_bytes=4 * mega),
        cost_estimate=cost(2 * half * vocab_local, 10 * half * vocab_local),
    )(total, token_weight, *parts)


def hidden_term(gap, weight):
    return lax.dot_general(
        gap[...], weight, (((1,), (1,)), ((), ())), preferred_element_type=jnp.float32
    )


def column_tiles(tile=256):
    return [slice(at, at + tile) for at in range(0, student_width, tile)]


def hidden_own_kernel(gap, weight, out):
    for cols in column_tiles():
        out[:, cols] = hidden_term(gap, weight[cols])


def hidden_own(gap, weight):
    return pl.pallas_call(
        hidden_own_kernel,
        in_specs=[whole()] * 2,
        out_specs=whole(),
        out_shape=jax.ShapeDtypeStruct((half, student_width), jnp.float32),
        compiler_params=pltpu.CompilerParams(vmem_limit_bytes=14 * mega),
        cost_estimate=cost(half * weight.size, 2 * weight.size),
    )(gap, weight)


def hidden_all_kernel(places, own, gap, weight, keep, send1, send2, send3, term):
    for cols in column_tiles():
        term[:half, cols] = own[:, cols]
        term[half:, cols] = hidden_term(gap, weight[cols])
        for pair in range(32):
            both = [term[placed(places, 1, 2 * pair + i), cols] for i in range(2)]
            both = jnp.concatenate(both, axis=0)
            out = (keep, send1, send2, send3)[pair // 8]
            at = 16 * (pair % 8)
            out[at : at + 16, cols] = both.astype(out.dtype)


def hidden_all(places, own, gap, weight):
    return pl.pallas_call(
        hidden_all_kernel,
        in_specs=[scalars()] + [whole()] * 3,
        out_specs=[whole()] * 4,
        out_shape=[jax.ShapeDtypeStruct((128, student_width), jnp.float32)]
        + [jax.ShapeDtypeStruct((128, student_width), jnp.bfloat16)] * 3,
        scratch_shapes=[pltpu.VMEM((tokens, student_width), jnp.float32)],
        compiler_params=pltpu.CompilerParams(vmem_limit_bytes=22 * mega),
        cost_estimate=cost(half * weight.size, 2 * weight.size),
    )(places, own, gap, weight)


def first_sum_kernel(mine, *refs):
    received, out = refs[:3], refs[3]
    for at in range(0, mine.shape[0], 16):
        rows = slice(at, at + 16)
        total = mine[rows] + sum(r[rows].astype(jnp.float32) for r in received)
        out[rows] = total.astype(out.dtype)


def first_sum(mine, received):
    return pl.pallas_call(
        first_sum_kernel,
        in_specs=[whole()] * 4,
        out_specs=whole(),
        out_shape=jax.ShapeDtypeStruct(mine.shape, jnp.bfloat16),
        compiler_params=pltpu.CompilerParams(vmem_limit_bytes=6 * mega),
        cost_estimate=cost(128 * student_width * 4, 2 * mega),
    )(mine, *received)


def last_sum_kernel(received, out):
    total = received[0].astype(jnp.float32)
    for i in range(1, received.shape[0]):
        total += received[i].astype(jnp.float32)
    out[...] = total.astype(out.dtype)


def last_sum(received):
    return pl.pallas_call(
        last_sum_kernel,
        in_specs=[whole()],
        out_specs=whole(),
        out_shape=jax.ShapeDtypeStruct(received.shape[1:], received.dtype),
        compiler_params=pltpu.CompilerParams(vmem_limit_bytes=3 * mega),
        cost_estimate=cost(received.size, 2 * received.size),
    )(received)


def grad_weight_kernel(rows, own, other, out):
    over_rows = (((0,), (0,)), ((), ()))
    out[...] = (
        lax.dot_general(rows[:half], own[...], over_rows, preferred_element_type=jnp.float32)
        + lax.dot_general(rows[half:], other[...], over_rows, preferred_element_type=jnp.float32)
    ).astype(jnp.bfloat16)


def grad_weight_of(rows, own, other, tile=256):
    return pl.pallas_call(
        grad_weight_kernel,
        grid=(student_width // tile,),
        in_specs=[pl.BlockSpec((tokens, tile), lambda j: (0, j)), whole(), whole()],
        out_specs=pl.BlockSpec((tile, vocab_local), lambda j: (j, 0)),
        out_shape=jax.ShapeDtypeStruct((student_width, vocab_local), jnp.bfloat16),
        compiler_params=pltpu.CompilerParams(vmem_limit_bytes=9 * mega),
        cost_estimate=cost(tokens * student_width * vocab_local, 2 * student_width * vocab_local),
    )(rows, own, other)


def local(hidden_teacher, hidden_student, teacher_weight, student_weight, token_weight):
    main_order, apart_order, places, first_core = setup(teacher_weight)

    def shared_along(block, axes):
        return [block] + [send(block, axes, by) for by in offsets[1:]]

    def joined(blocks):
        return jnp.concatenate(blocks, axis=0)

    block = joined(shared_along(side_by_side(hidden_teacher, hidden_student), main_axes[0]))
    block, places = lax.optimization_barrier((block, places))
    separate, main = block[:, :apart], block[:, apart:]
    main, separate = shared_along(main, main_axes[1]), shared_along(separate, apart_axes[1])
    main = joined(main)
    _, *separate = lax.optimization_barrier((main, *separate))
    separate = joined(separate)
    main = shared_along(main, main_axes[2])
    separate = shared_along(separate, apart_axes[2])
    early = teacher_early(main[0], teacher_weight)
    teacher_own, teacher_other = teacher_logits(places, early, main[1:], teacher_weight)
    teacher_other, *separate = lax.optimization_barrier((teacher_other, *separate))
    teacher_other = swap(teacher_other)
    cols = 1024
    own0, other0, rows = student_logits(
        main_order, apart_order, main, separate, student_weight, cols
    )
    other0 = swap(other0)
    own1, other1 = student_rest(rows, student_weight, vocab_local - cols)
    teacher_own, other1 = lax.optimization_barrier((teacher_own, other1))
    other1 = swap(other1)
    teacher = teacher_statistics(teacher_own, teacher_other)
    student_part0, teacher_part0, sums = student_statistics(teacher, (own0, other0), 0)
    student_part1, teacher_part1, sums = student_statistics(teacher, (own1, other1), cols, sums)
    for axes in reduce_axes:
        sums = sum(shared_along(sums, axes))
    gap, divergence = gap_of(
        sums, token_weight.reshape(4, 128), (student_part0, teacher_part0, student_part1, teacher_part1)
    )
    gap_other, divergence_other = lax.optimization_barrier((swap(gap), swap(divergence)))

    def sent_back(sends, axes):
        far = send(sends[2], axes, -offsets[3])
        return [send(b, axes, -by) for b, by in zip(sends[:2], offsets[1:3])] + [far]

    hidden = hidden_own(gap, student_weight)
    gap_other, hidden = lax.optimization_barrier((gap_other, hidden))
    keep, *sends = hidden_all(places, hidden, gap_other, student_weight)
    received = sent_back(sends, reduce_axes[0])
    grad_weight = grad_weight_of(rows, gap, gap_other)
    keep, grad_weight = lax.optimization_barrier((keep, grad_weight))
    total = first_sum(keep, received).reshape(16, 8, student_width)
    total = lax.all_to_all(total, everyone, 0, 0, axis_index_groups=planes())
    grad_hidden = last_sum(total)

    first_core = first_core > 0.5
    divergence = jnp.concatenate(
        [
            jnp.where(first_core, divergence, divergence_other),
            jnp.where(first_core, divergence_other, divergence),
        ]
    ).reshape(tokens)
    return (divergence, grad_hidden, grad_weight)


def solution(mesh):
    placed = (
        P(("batch", "vocab"), "mp"),
        P(("batch", "vocab"), "mp"),
        P("mp", ("batch", "vocab")),
        P("mp", ("batch", "vocab")),
        P(),
    )
    return jax.shard_map(
        local,
        mesh=mesh,
        in_specs=placed,
        out_specs=(P(), P(("batch", "vocab"), "mp"), P("mp", ("batch", "vocab"))),
        check_vma=False,
    )
```
